32 devices in a mesh: groups: 2 (over y), segment: 8 (over z, x), template: 2 (over core).
Axes of the slice: x: 2, y: 2, z: 4, core: 2. Of those that a mesh axis runs over, the one named last changes fastest.
Arguments:
- strain_frames: bfloat16 [64, 16384], P('segment'), may hold values from -6 to 6
- frame_slot: int32 [8, 8], replicated, may hold values from 0 to 7, as said below
- templates: bfloat16 [4, 2, 131072], P(('groups', 'template'), None, 'segment'), parts along dimension 0, may hold values from -6 to 6
- bin_edges: int32 [4, 3], P(('groups', 'template')), parts along dimension 0, may hold values from 16384 to 114687, as said below
Outputs:
- snr_series: bfloat16 [8, 4, 131072], P('segment', ('groups', 'template')), parts along dimension 1
- chisq_series: bfloat16 [8, 4, 131072], P('segment', ('groups', 'template')), parts along dimension 1
- peak_newsnr: float32 [8, 4], P('segment', ('groups', 'template')), parts along dimension 1
The draws below stay inside these ranges and needn't reach their ends.
There are 2 independent parts, one for each index of `groups`. The reference program is written for one: setup_inputs(seed, part) draws one part's arguments, and reference() takes and returns one part's arrays. A program takes and returns all parts, laid end to end along the dimension named above; an argument that names none is the same for every part. Nothing has to cross between parts.
Inputs may be any that keep to these rules, and one draw needn't show every extreme that they name: Each column frame_slot[:, j] is a permutation of 0 to 7. `bin_edges`: edge number e of a template lies in [(2 e + 1) * 16384, (2 e + 3) * 16384), so the edges rise.
All inputs are finite; a program needn't handle non-finite values.
Results may differ from the reference program's by a relative error of at most 0.011.
Values may be sent and summed in bfloat16 or wider, within the bound.
No kernel may reach another device: no remote copies, remote signals or barrier semaphores. Data moves between devices by JAX's collectives and lax.ppermute only.
A program may use at most 64 MiB of HBM per device.

```python
import math
import jax
import jax.numpy as jnp
from jax import lax

RADIX_A = 64
RADIX_B = 32
RADIX_C = 128
KB = 131072
NSEG = 8
FRAMELEN = 16384
FRAMES = 64
TEMPLATES = 2


def shuffle_column(single_key):
    return jax.random.permutation(single_key, NSEG)


def draw_frame_slot(key, part):
    column_keys = jax.random.split(key, NSEG)
    columns = jax.vmap(shuffle_column)(column_keys)
    return jnp.transpose(columns).astype(jnp.int32)


def draw_bin_edges(key, part):
    offsets = jax.random.randint(key, (TEMPLATES, 3), 0, KB // 4)
    offsets = offsets.at[0, 0].set(0)
    offsets = offsets.at[TEMPLATES - 1, 2].set(KB // 4 - 1)
    bases = KB // 8 * jnp.array([1, 3, 5], dtype=jnp.int32)
    return (offsets + bases[None, :]).astype(jnp.int32)


def shard_levels(stream_key, shape, cuts, smallest, largest):
    def one(dim, shards_of):
        steps = jax.random.uniform(jax.random.fold_in(jax.random.fold_in(stream_key, 6), dim), (shards_of,), jnp.float32, smallest / len(cuts), largest / len(cuts))
        return jnp.repeat(jnp.exp(steps), shape[dim] // shards_of).reshape((-1,) + (1,) * (len(shape) - dim - 1))

    loudness = one(*cuts[0])
    for cut in cuts[1:]:
        loudness = loudness * one(*cut)
    return loudness


def normal_values(own_key, extent, deviation, limit, cuts=(), held_as=jnp.bfloat16):
    loudness = shard_levels(own_key, extent, cuts, -0.22, 0.18) if cuts else 1.0
    values = jax.random.normal(own_key, extent, jnp.float32) * deviation * loudness
    return jnp.minimum(jnp.maximum(values, -limit), limit).astype(held_as)


def setup_inputs(seed: int = 0, part: int = 0) -> dict:
    keys = jax.random.split(jax.random.key(seed), 5)
    part_splits = jax.random.split(jax.random.fold_in(keys[4], part), 5)
    return {
        "strain_frames": normal_values(keys[0], (FRAMES, FRAMELEN), 1.0, 6.0, ((0, 8),)),
        "frame_slot": draw_frame_slot(jax.random.fold_in(keys[4], 71), part),
        "templates": normal_values(part_splits[2], (TEMPLATES, 2, KB), 1.0, 6.0, ((0, 2), (2, 8))),
        "bin_edges": draw_bin_edges(jax.random.fold_in(jax.random.fold_in(keys[4], part), 71), part),
    }


def dft_table(length, orient):
    counter = jnp.arange(length, dtype=jnp.int32)
    product = counter[:, None] * counter[None, :] % length
    angles = orient * 2.0 * math.pi / length * product.astype(jnp.float32)
    cosine = jnp.cos(angles)
    sine = jnp.sin(angles)
    upper = jnp.stack([cosine, -sine], axis=1)
    lower = jnp.stack([sine, cosine], axis=1)
    return jnp.stack([upper, lower], axis=0).astype(jnp.bfloat16)

def rotate(values, phase_index, modulus, orient):
    angles = orient * 2.0 * math.pi / modulus * (phase_index % modulus).astype(jnp.float32)
    cosine = jnp.cos(angles)
    sine = jnp.sin(angles)
    real_part = values[0] * cosine - values[1] * sine
    imag_part = values[0] * sine + values[1] * cosine
    return jnp.stack([real_part, imag_part]).astype(jnp.bfloat16)

def product_level(form, table, values):
    return jnp.einsum(form, table.astype(jnp.float32), values.astype(jnp.float32), precision=lax.Precision.HIGHEST)

def transform(signal, orient):
    length = RADIX_A * RADIX_B * RADIX_C
    inner = RADIX_B * RADIX_C
    start = signal.reshape(2, RADIX_A, inner)
    level_one = product_level('ckdp,dpq->ckq', dft_table(RADIX_A, orient), start)
    grid_one = jnp.arange(RADIX_A, dtype=jnp.int32)[:, None] * jnp.arange(inner, dtype=jnp.int32)[None, :]
    turned = rotate(level_one, grid_one, length, orient).reshape(2, RADIX_A, RADIX_B, RADIX_C)
    level_two = product_level('cjdp,dkpr->ckjr', dft_table(RADIX_B, orient), turned)
    grid_two = jnp.arange(RADIX_B, dtype=jnp.int32)[:, None] * jnp.arange(RADIX_C, dtype=jnp.int32)[None, :]
    turned_two = rotate(level_two, grid_two, inner, orient)
    level_three = product_level('cldr,dkjr->ckjl', dft_table(RADIX_C, orient), turned_two)
    return jnp.transpose(level_three, (0, 3, 2, 1)).reshape(2, length)

def filter_template(spectrum, template, edges):
    length = RADIX_A * RADIX_B * RADIX_C
    kept = length // 2
    temp_real = template[0].astype(jnp.float32)
    temp_imag = template[1].astype(jnp.float32)
    corr_real = spectrum[0] * temp_real + spectrum[1] * temp_imag
    corr_imag = spectrum[1] * temp_real - spectrum[0] * temp_imag
    power = temp_real * temp_real + temp_imag * temp_imag
    total = jnp.sum(power)
    bin_index = jnp.arange(kept, dtype=jnp.int32)
    label = (bin_index >= edges[0]).astype(jnp.int32) + (bin_index >= edges[1]).astype(jnp.int32) + (bin_index >= edges[2]).astype(jnp.int32)
    padding = jnp.zeros((2, length - kept), jnp.bfloat16)
    pieces = []
    shares = []
    for number in range(4):
        inside = (label == number).astype(jnp.float32)
        shares.append(jnp.sum(power * inside) / total)
        masked = jnp.stack([corr_real * inside, corr_imag * inside]).astype(jnp.bfloat16)
        series = transform(jnp.concatenate([masked, padding], axis=1), 1.0) / length
        pieces.append(series[:, length // 4:length // 4 + kept])
    summed = pieces[0] + pieces[1] + pieces[2] + pieces[3]
    scale = length / total
    snr = jnp.sqrt((summed[0] * summed[0] + summed[1] * summed[1]) * scale)
    chisq = jnp.zeros_like(snr)
    for number in range(4):
        diff_real = pieces[number][0] - shares[number] * summed[0]
        diff_imag = pieces[number][1] - shares[number] * summed[1]
        chisq = chisq + diff_real * diff_real + diff_imag * diff_imag
    chisq = chisq * scale
    reduced = chisq / 6.0
    weighted = snr * ((1.0 + reduced * reduced * reduced) / 2.0) ** (-1.0 / 6.0)
    newsnr = jnp.where(reduced > 1.0, weighted, snr)
    return (snr.astype(jnp.bfloat16), chisq.astype(jnp.bfloat16), jnp.max(newsnr))

def reference(strain_frames, frame_slot, templates, bin_edges):
    count = frame_slot.shape[0]
    frame_length = strain_frames.shape[1]
    length = RADIX_A * RADIX_B * RADIX_C
    kept = length // 2
    grouped = strain_frames.reshape(count, count, frame_length)

    def gather_half(half):
        column = lax.dynamic_index_in_dim(frame_slot, half, 1, keepdims=False)
        order = jnp.argsort(column, stable=True).astype(jnp.int32)
        owned = lax.dynamic_index_in_dim(grouped, half, 1, keepdims=False)
        return owned[order].reshape(kept)
    halves = lax.map(gather_half, jnp.arange(count, dtype=jnp.int32))
    padded = jnp.concatenate([halves, jnp.zeros((1, kept), jnp.bfloat16)], axis=0)

    def one_segment(index):
        window = lax.dynamic_slice_in_dim(padded, index, 2, 0).reshape(length)
        signal = jnp.stack([window, jnp.zeros_like(window)])
        spectrum = transform(signal, -1.0)[:, :kept]

        def one_template(number):
            template = lax.dynamic_index_in_dim(templates, number, 0, keepdims=False)
            edges = lax.dynamic_index_in_dim(bin_edges, number, 0, keepdims=False)
            return filter_template(spectrum, template, edges)
        return lax.map(one_template, jnp.arange(templates.shape[0], dtype=jnp.int32))
    snr_series, chisq_series, peak_newsnr = lax.map(one_segment, jnp.arange(count, dtype=jnp.int32))
    return (snr_series, chisq_series, peak_newsnr)
```

```python
import math

import jax
import jax.numpy as jnp
import ml_dtypes
import numpy as np
from jax import lax
from jax.experimental import pallas as pl
from jax.experimental.pallas import tpu as pltpu
from jax.sharding import PartitionSpec as P

SIDE = 512
HALF = SIDE // 2
LENGTH = SIDE * SIDE
AXES = ("groups", "segment", "template")
MIB = 1 << 20
BIN_LOW = (0, 32, 96, 128)


def turn(rows, columns, modulus):
    product = np.outer(rows, columns) % modulus
    angles = 2.0 * math.pi / modulus * product.astype(np.float64)
    return np.cos(angles), np.sin(angles)


def tables():
    digit = np.arange(SIDE)
    cosine, sine = turn(digit, digit, SIDE)
    first = np.concatenate([cosine, -sine], axis=0)
    low = slice(0, HALF)
    second = np.block([[cosine[:, low], -sine[:, low]], [sine[:, low], cosine[:, low]]])
    third = []
    column = np.arange(HALF // 2)
    for start in BIN_LOW:
        chosen = np.where(column >= start, column, column + HALF // 2)
        third.append(
            np.block([[cosine[chosen], sine[chosen]], [-sine[chosen], cosine[chosen]]])
        )
    kept = slice(HALF // 2, HALF // 2 + HALF)
    fourth = np.block([[cosine[kept], -sine[kept]], [sine[kept], cosine[kept]]])
    phase_cos, phase_sin = turn(digit, digit, LENGTH)
    phase = np.stack([phase_cos, phase_sin]).astype(np.float32)


    narrow = [x.astype(np.float32).astype(ml_dtypes.bfloat16) for x in (first, second, np.stack(third), fourth)]
    return (*narrow, phase)


def in_vmem(*arrays):
    return [pltpu.with_memory_space_constraint(x, pltpu.VMEM) for x in arrays]


def split_frames(frames):
    count, samples = frames.shape
    rows = samples // SIDE
    tiles = SIDE // 128

    def body(frames_ref, out_ref, wide):
        core = lax.axis_index("template")
        wide[:, count * rows :, :] = jnp.zeros((tiles, rows, 128), jnp.float32)
        for row in range(rows):
            for tile in range(tiles):
                place = (row * tiles + tile) * 128
                wide[tile, pl.ds(row, count, stride=rows), :] = frames_ref[
                    :, place : place + 128
                ].astype(jnp.float32)
        for tile in range(tiles):
            moved = wide[tile, pl.ds(pl.multiple_of(core * rows, rows), count * rows), :]
            out_ref[:, :, tile * 128 : tile * 128 + 128] = moved.astype(jnp.bfloat16).reshape(
                count, rows, 128
            )

    return pl.pallas_call(
        body,
        out_shape=pltpu.VMEM((count, rows, SIDE), jnp.bfloat16),
        in_specs=[pl.BlockSpec(memory_space=pltpu.VMEM)],
        out_specs=pl.BlockSpec(memory_space=pltpu.VMEM),
        scratch_shapes=[pltpu.VMEM((tiles, (count + 1) * rows, 128), jnp.float32)],
        compiler_params=pltpu.CompilerParams(vmem_limit_bytes=16 * MIB),
        name="split_frames",
    )(frames)


def forward_body(signal, first, second, phase, spectrum, turned):
    rows = SIDE // 2

    def chunk(index, carry):
        here = pl.ds(pl.multiple_of(index * rows, rows), rows)
        there = pl.ds(pl.multiple_of(SIDE + index * rows, rows), rows)
        real = jnp.dot(first[here, :], signal[...], preferred_element_type=jnp.float32)
        imag = jnp.dot(first[there, :], signal[...], preferred_element_type=jnp.float32)
        cosine, sine = phase[0, here, :], phase[1, here, :]
        turned[here, :SIDE] = (real * cosine + imag * sine).astype(jnp.bfloat16)
        turned[here, SIDE:] = (imag * cosine - real * sine).astype(jnp.bfloat16)
        spectrum[here, :] = jnp.dot(
            turned[here, :], second[...], preferred_element_type=jnp.float32
        )
        return carry

    lax.fori_loop(0, SIDE // rows, chunk, 0)


def forward_received(own, other, frame_slot, first, second, phase):
    count, rows, _ = own.shape

    def body(own_ref, other_ref, slot_ref, first_ref, second_ref, phase_ref, spectrum, signal, turned):
        segment = lax.axis_index("segment")
        core = lax.axis_index("template")
        for part, frames in ((core, own_ref), (1 - core, other_ref)):
            half = jnp.minimum(segment + part, count - 1)
            for source in range(count):
                start = part * HALF + slot_ref[source, half] * rows
                signal[pl.ds(pl.multiple_of(start, rows), rows), :] = frames[source]
        forward_body(signal, first_ref, second_ref, phase_ref, spectrum, turned)

    vmem = pl.BlockSpec(memory_space=pltpu.VMEM)
    return pl.pallas_call(
        body,
        out_shape=pltpu.VMEM((SIDE, SIDE), jnp.float32),
        in_specs=[vmem, vmem, pl.BlockSpec(memory_space=pltpu.SMEM), vmem, vmem, vmem],
        out_specs=vmem,
        scratch_shapes=[
            pltpu.VMEM((SIDE, SIDE), jnp.bfloat16),
            pltpu.VMEM((SIDE, 2 * SIDE), jnp.bfloat16),
        ],
        compiler_params=pltpu.CompilerParams(vmem_limit_bytes=32 * MIB),
        cost_estimate=pl.CostEstimate(
            flops=4 * SIDE**3 * 2, bytes_accessed=6 * MIB, transcendentals=0
        ),
        name="forward",
    )(own, other, frame_slot, *in_vmem(first, second, phase))


def forward_arranged(signal, first, second, phase):
    def body(signal_ref, first_ref, second_ref, phase_ref, spectrum, turned):
        forward_body(signal_ref, first_ref, second_ref, phase_ref, spectrum, turned)

    vmem = pl.BlockSpec(memory_space=pltpu.VMEM)
    return pl.pallas_call(
        body,
        out_shape=pltpu.VMEM((SIDE, SIDE), jnp.float32),
        in_specs=[vmem] * 4,
        out_specs=vmem,
        scratch_shapes=[pltpu.VMEM((SIDE, 2 * SIDE), jnp.bfloat16)],
        compiler_params=pltpu.CompilerParams(vmem_limit_bytes=32 * MIB),
        name="forward",
    )(signal, *in_vmem(first, second, phase))


def owners_of(segment, core, doubled):
    if not doubled:
        return [[0]]
    near, far = 2 - core, 1 + core
    masks = [[0], [4], [near, near ^ 4], [far, far ^ 4, far ^ near, far ^ near ^ 4]]
    return [[segment ^ mask for mask in block] for block in masks]


def inverse(spectrum, blocks, edges, third, fourth, phase, doubled):
    n_blocks = len(blocks)
    shard = blocks[0].shape[2]
    quarter = HALF // 2
    rows = SIDE // 2
    wide = SIDE // 2

    def body(*refs):
        spectrum_ref, block_refs = refs[0], refs[1 : 1 + n_blocks]
        edge_ref, third_ref, fourth_ref, phase_ref = refs[1 + n_blocks : 5 + n_blocks]
        snr_ref, chisq_ref, peak_ref = refs[5 + n_blocks : 8 + n_blocks]
        gathered, flipped, masked, turned, sums = refs[8 + n_blocks :]
        segment = lax.axis_index("segment")
        core = lax.axis_index("template")
        for block, owners in zip(block_refs, owners_of(segment, core, doubled), strict=True):
            for place, owner in enumerate(owners):
                here = pl.ds(pl.multiple_of(owner * shard, shard), shard)
                for part in range(2):
                    gathered[part, here, :] = block[place, part]
        for part in range(2):
            flipped[:, part * HALF : (part + 1) * HALF] = gathered[part].T
        edge = [edge_ref[0, number] for number in range(3)]
        sums[...] = jnp.zeros_like(sums)
        step = 32

        def correlate(index, carry):
            here = pl.ds(pl.multiple_of(index * step, step), step)
            spec_real = [spectrum_ref[here, q * quarter : (q + 1) * quarter] for q in range(2)]
            spec_imag = [spectrum_ref[here, (q + 2) * quarter : (q + 3) * quarter] for q in range(2)]
            temp_real = [
                flipped[here, q * quarter : (q + 1) * quarter].astype(jnp.float32) for q in range(2)
            ]
            temp_imag = [
                flipped[here, (q + 2) * quarter : (q + 3) * quarter].astype(jnp.float32)
                for q in range(2)
            ]
            lane = lax.broadcasted_iota(jnp.int32, (step, quarter), 1)
            base = lane * SIDE + lax.broadcasted_iota(jnp.int32, (step, quarter), 0) + index * step
            zero = jnp.zeros((step, quarter), jnp.float32)
            corr, above, power = [], [], []
            for q in range(2):
                corr.append(
                    (
                        spec_real[q] * temp_real[q] + spec_imag[q] * temp_imag[q],
                        spec_imag[q] * temp_real[q] - spec_real[q] * temp_imag[q],
                    )
                )
                power.append(temp_real[q] * temp_real[q] + temp_imag[q] * temp_imag[q])
                bins = base + q * quarter * SIDE
                above.append([bins >= edge[number] for number in range(3)])
            inside = [
                [~above[0][0], None],
                [above[0][0] & ~above[0][1], ~above[1][1]],
                [above[0][1] & ~above[0][2], above[1][1] & ~above[1][2]],
                [None, above[1][2]],
            ]
            inside[1][1] = ~above[1][1] & above[1][0]
            for number in range(4):
                first_half, second_half = inside[number]
                if second_half is None:
                    chosen = [jnp.where(first_half, corr[0][part], zero) for part in range(2)]
                    strength = jnp.where(first_half, power[0], zero)
                elif first_half is None:
                    chosen = [jnp.where(second_half, corr[1][part], zero) for part in range(2)]
                    strength = jnp.where(second_half, power[1], zero)
                else:
                    chosen = [
                        jnp.where(
                            first_half, corr[0][part], jnp.where(second_half, corr[1][part], zero)
                        )
                        for part in range(2)
                    ]
                    strength = jnp.where(first_half, power[0], zero) + jnp.where(
                        second_half, power[1], zero
                    )
                for part in range(2):
                    masked[number, here, part * quarter : (part + 1) * quarter] = chosen[
                        part
                    ].astype(jnp.bfloat16)
                folded = strength[0:8]
                for start in range(8, step, 8):
                    folded = folded + strength[start : start + 8]
                sums[number] += folded
            return carry

        lax.fori_loop(0, SIDE // step, correlate, 0)

        def first_pass(index, carry):
            number, part = index // (SIDE // rows), index % (SIDE // rows)
            here = pl.ds(pl.multiple_of(part * rows, rows), rows)
            there = pl.ds(pl.multiple_of(SIDE + part * rows, rows), rows)
            product = jnp.dot(
                masked[number, here, :], third_ref[number], preferred_element_type=jnp.float32
            )
            real, imag = product[:, :SIDE], product[:, SIDE:]
            cosine, sine = phase_ref[0, here, :], phase_ref[1, here, :]
            turned[number, here, :] = (real * cosine - imag * sine).astype(jnp.bfloat16)
            turned[number, there, :] = (real * sine + imag * cosine).astype(jnp.bfloat16)
            return carry

        lax.fori_loop(0, 4 * (SIDE // rows), first_pass, 0)

        bin_power = [jnp.sum(sums[number]) for number in range(4)]
        total = (bin_power[0] + bin_power[1]) + (bin_power[2] + bin_power[3])
        total_row = jnp.full((1, wide), total, jnp.float32)
        shares = [jnp.full((1, wide), bin_power[number], jnp.float32) / total_row for number in range(4)]
        scale = (1.0 / LENGTH) / total_row

        def second_pass(index, peak):
            columns = pl.ds(pl.multiple_of(index * wide, wide), wide)
            pieces = [
                jnp.dot(
                    fourth_ref[...], turned[number, :, columns], preferred_element_type=jnp.float32
                )
                for number in range(4)
            ]
            real = [piece[:HALF] for piece in pieces]
            imag = [piece[HALF:] for piece in pieces]
            sum_real = (real[0] + real[1]) + (real[2] + real[3])
            sum_imag = (imag[0] + imag[1]) + (imag[2] + imag[3])
            snr = jnp.sqrt((sum_real * sum_real + sum_imag * sum_imag) * scale)
            chisq = jnp.zeros_like(snr)
            for number in range(4):
                diff_real = real[number] - shares[number] * sum_real
                diff_imag = imag[number] - shares[number] * sum_imag
                chisq = chisq + (diff_real * diff_real + diff_imag * diff_imag)
            chisq = chisq * scale
            reduced = chisq / 6.0
            inner = (1.0 + reduced * reduced * reduced) / 2.0
            weighted = snr * jnp.exp(jnp.log(inner) * (-1.0 / 6.0))
            newsnr = jnp.where(reduced > 1.0, weighted, snr)
            snr_ref[:, columns] = snr.astype(jnp.bfloat16)
            chisq_ref[:, columns] = chisq.astype(jnp.bfloat16)
            return jnp.maximum(peak, jnp.max(newsnr, axis=0, keepdims=True))

        peak = lax.fori_loop(
            0, SIDE // wide, second_pass, jnp.zeros((1, wide), jnp.float32)
        )
        peak_ref[...] = jnp.max(peak, axis=1, keepdims=True)

    vmem = pl.BlockSpec(memory_space=pltpu.VMEM)
    return pl.pallas_call(
        body,
        out_shape=(
            jax.ShapeDtypeStruct((HALF, SIDE), jnp.bfloat16),
            jax.ShapeDtypeStruct((HALF, SIDE), jnp.bfloat16),
            jax.ShapeDtypeStruct((1, 1), jnp.float32),
        ),
        in_specs=[vmem] * (1 + n_blocks) + [pl.BlockSpec(memory_space=pltpu.SMEM)] + [vmem] * 3,
        out_specs=(vmem, vmem, vmem),
        scratch_shapes=[
            pltpu.VMEM((2, HALF, SIDE), jnp.bfloat16),
            pltpu.VMEM((SIDE, SIDE), jnp.bfloat16),
            pltpu.VMEM((4, SIDE, HALF), jnp.bfloat16),
            pltpu.VMEM((4, 2 * SIDE, SIDE), jnp.bfloat16),
            pltpu.VMEM((4, 8, quarter), jnp.float32),
        ],
        compiler_params=pltpu.CompilerParams(vmem_limit_bytes=48 * MIB),
        name="inverse",
    )(spectrum, *blocks, edges, *in_vmem(third, fourth, phase))


def partner(mesh_shape, mask_of):
    groups, segments, cores = (mesh_shape[name] for name in AXES)
    pairs = []
    for group in range(groups):
        for segment in range(segments):
            for core in range(cores):
                here = (group * segments + segment) * cores + core
                other = segment ^ mask_of(core)
                pairs.append((here, (group * segments + other) * cores + core))
    return pairs


def gather_doubling(shard, mesh_shape):
    across = lax.ppermute(shard, AXES, partner(mesh_shape, lambda core: 4))
    pair = jnp.concatenate([shard, across])
    near = lax.ppermute(pair, AXES, partner(mesh_shape, lambda core: 2 - core))
    four = jnp.concatenate([pair, near])
    far = lax.ppermute(four, AXES, partner(mesh_shape, lambda core: 1 + core))
    return [shard, across, near, far]


def arrange_plain(strain_frames, frame_slot):
    count = lax.axis_size("segment")
    position = lax.axis_index("segment")
    frame_length = strain_frames.shape[1]
    counter = jnp.arange(count, dtype=jnp.int32)
    slot_now = lax.dynamic_slice_in_dim(frame_slot, position, 1, 1)[:, 0]
    next_index = jnp.minimum(position + 1, count - 1)
    slot_next = lax.dynamic_slice_in_dim(frame_slot, next_index, 1, 1)[:, 0]

    def arrange(slots, frames):
        selector = (counter[:, None] == slots[None, :]).astype(jnp.bfloat16)
        placed = jnp.dot(selector, frames, preferred_element_type=jnp.float32)
        return placed.astype(jnp.bfloat16).reshape(HALF, SIDE)

    following_rows = jnp.concatenate(
        [strain_frames[1:], jnp.zeros((1, frame_length), jnp.bfloat16)], axis=0
    )
    outgoing = jnp.stack([strain_frames, following_rows], axis=1)
    received = lax.all_to_all(outgoing, "segment", split_axis=0, concat_axis=0, tiled=True)
    leading = arrange(slot_now, received[:, 0])
    trailing = arrange(slot_next, received[:, 1])
    return jnp.concatenate([leading, trailing])


def local(mesh_shape, strain_frames, frame_slot, templates, bin_edges):
    first, second, third, fourth, phase = tables()
    count = mesh_shape["segment"]
    rows = strain_frames.shape[1] // SIDE
    staged = count == 8 and mesh_shape["template"] == 2 and rows % 16 == 0
    if staged:
        shard = templates.reshape(1, 2, -1, SIDE)
        blocks = gather_doubling(shard, mesh_shape)
        outgoing = split_frames(strain_frames)
        own = lax.all_to_all(outgoing, "segment", split_axis=0, concat_axis=0, tiled=True)
        other = lax.ppermute(own, "template", [(0, 1), (1, 0)])
        spectrum = forward_received(own, other, frame_slot, first, second, phase)
    else:
        signal = arrange_plain(strain_frames, frame_slot)
        whole = lax.all_gather(templates, "segment", axis=2, tiled=True)
        blocks = [whole.reshape(1, 2, HALF, SIDE)]
        spectrum = forward_arranged(signal, first, second, phase)
    snr, chisq, peak = inverse(spectrum, blocks, bin_edges, third, fourth, phase, staged)
    return snr.reshape(1, 1, LENGTH // 2), chisq.reshape(1, 1, LENGTH // 2), peak


def solution(mesh):
    mesh_shape = dict(mesh.shape)

    def step(strain_frames, frame_slot, templates, bin_edges):
        return local(mesh_shape, strain_frames, frame_slot, templates, bin_edges)

    in_specs = (
        P("segment", None),
        P(),
        P(("groups", "template"), None, "segment"),
        P(("groups", "template"), None),
    )
    out_specs = (
        P("segment", ("groups", "template"), None),
        P("segment", ("groups", "template"), None),
        P("segment", ("groups", "template")),
    )
    return jax.shard_map(step, mesh=mesh, in_specs=in_specs, out_specs=out_specs, check_vma=False)
```

```python
import functools
import math

import jax
import jax.numpy as jnp
import ml_dtypes
import numpy as np
from jax import lax
from jax.experimental import pallas as pl
from jax.experimental.pallas import tpu as pltpu
from jax.sharding import PartitionSpec as P

SIDE = 512
HALF = SIDE // 2
LENGTH = SIDE * SIDE
AXES = ("groups", "segment", "template")
MIB = 1 << 20
BIN_LOW = (0, 32, 96, 128)
ROUNDS = 4


def strain_mask(step, core):
    if isinstance(core, int):
        return (step + 1) % ROUNDS if core == 0 else step + ROUNDS
    return jnp.where(core == 0, (step + 1) % ROUNDS, step + ROUNDS)


def turn(rows, columns, modulus):
    product = np.outer(rows, columns) % modulus
    angles = 2.0 * math.pi / modulus * product.astype(np.float64)
    return np.cos(angles), np.sin(angles)


def tables():
    digit = np.arange(SIDE)
    cosine, sine = turn(digit, digit, SIDE)
    first = np.concatenate([cosine, -sine], axis=0)
    low = slice(0, HALF)
    second = np.block([[cosine[:, low], -sine[:, low]], [sine[:, low], cosine[:, low]]])
    third = []
    column = np.arange(HALF // 2)
    for start in BIN_LOW:
        chosen = np.where(column >= start, column, column + HALF // 2)
        third.append(
            np.block([[cosine[chosen], sine[chosen]], [-sine[chosen], cosine[chosen]]])
        )
    fourth = []
    for parity in range(2):
        kept = slice(HALF // 2 + parity, HALF // 2 + HALF, 2)
        fourth.append(
            np.block(
                [[cosine[kept, low], -sine[kept, low]], [sine[kept, low], cosine[kept, low]]]
            )
        )
    phase_cos, phase_sin = turn(digit, digit, LENGTH)
    phase = np.stack([phase_cos, phase_sin]).astype(np.float32)


    narrow = [x.astype(np.float32).astype(ml_dtypes.bfloat16) for x in (first, second, np.stack(third), np.stack(fourth))]
    return (*narrow, phase)


def spread(source, wide, count, rows):
    tiles = SIDE // 128
    for row in range(rows):
        for tile in range(tiles):
            place = (row * tiles + tile) * 128
            wide[tile, pl.ds(row, count, stride=rows), :] = source[:, place : place + 128].astype(
                jnp.float32
            )


def split_frames(frames, shard):
    count, samples = frames.shape
    rows = samples // SIDE
    tiles = SIDE // 128

    def body(frames_ref, shard_ref, *refs):
        outs, unpacked, wide, narrow = refs[: ROUNDS + 1], *refs[ROUNDS + 1 :]
        segment = lax.axis_index("segment")
        core = lax.axis_index("template")
        wide[:, count * rows :, :] = jnp.zeros((tiles, rows, 128), jnp.float32)
        spread(frames_ref, wide, count, rows)
        for step, out_ref in enumerate(outs):
            mask = strain_mask(step, core) if step < ROUNDS else 0
            start = pl.multiple_of((segment ^ mask) * rows, rows)
            for tile in range(tiles):
                out_ref[:, :, tile * 128 : tile * 128 + 128] = (
                    wide[tile, pl.ds(start, 2 * rows), :].astype(jnp.bfloat16).reshape(2, rows, 128)
                )
        unpack(shard_ref, narrow, unpacked.at[0])

    vmem = pl.BlockSpec(memory_space=pltpu.VMEM)
    return pl.pallas_call(
        body,
        out_shape=[pltpu.VMEM((2, rows, SIDE), jnp.bfloat16)] * (ROUNDS + 1)
        + [pltpu.VMEM((1, 2, rows, SIDE), jnp.bfloat16)],
        in_specs=[vmem, vmem],
        out_specs=[vmem] * (ROUNDS + 2),
        scratch_shapes=[
            pltpu.VMEM((tiles, (count + 1) * rows, 128), jnp.float32),
            pltpu.VMEM((tiles, 2 * rows, 128), jnp.float32),
        ],
        compiler_params=pltpu.CompilerParams(vmem_limit_bytes=4 * MIB),
        name="split_frames",
    )(frames, shard)


def unpack(shard_ref, narrow, out_ref):
    rows = out_ref.shape[1]
    spread(shard_ref.at[0], narrow, 2, rows)
    for tile in range(SIDE // 128):
        out_ref[:, :, tile * 128 : tile * 128 + 128] = (
            narrow[tile].astype(jnp.bfloat16).reshape(2, rows, 128)
        )


def pair_shards(unpacked, across):
    rows = unpacked.shape[2]

    def body(unpacked_ref, across_ref, out_ref, narrow):
        out_ref[0] = unpacked_ref[0]
        unpack(across_ref, narrow, out_ref.at[1])

    vmem = pl.BlockSpec(memory_space=pltpu.VMEM)
    return pl.pallas_call(
        body,
        out_shape=pltpu.VMEM((2, 2, rows, SIDE), jnp.bfloat16),
        in_specs=[vmem, vmem],
        out_specs=vmem,
        scratch_shapes=[pltpu.VMEM((SIDE // 128, 2 * rows, 128), jnp.float32)],
        compiler_params=pltpu.CompilerParams(vmem_limit_bytes=4 * MIB),
        name="pair_shards",
    )(unpacked, across)


def load_tables(arrays, after):
    count = len(arrays)

    def body(*refs):
        sources, outs, arrived = refs[:count], refs[count + 1 : 2 * count + 1], refs[-1]
        copies = [
            pltpu.make_async_copy(source, out, arrived.at[place])
            for place, (source, out) in enumerate(zip(sources, outs, strict=True))
        ]
        for copy in copies:
            copy.start()
        for copy in copies:
            copy.wait()

    hbm = pl.BlockSpec(memory_space=pl.ANY)
    return pl.pallas_call(
        body,
        out_shape=[pltpu.VMEM(x.shape, x.dtype) for x in arrays],
        in_specs=[hbm] * (count + 1),
        out_specs=[pl.BlockSpec(memory_space=pltpu.VMEM)] * count,
        scratch_shapes=[pltpu.SemaphoreType.DMA((count,))],
        compiler_params=pltpu.CompilerParams(vmem_limit_bytes=1 * MIB),
        cost_estimate=pl.CostEstimate(flops=0, bytes_accessed=12 * MIB, transcendentals=0),
        name="load_tables",
    )(*(pltpu.with_memory_space_constraint(x, pltpu.HBM) for x in arrays), after)


def forward_body(signal, first, second, phase, spectrum, turned):
    rows = SIDE // 2

    def chunk(index, carry):
        here = pl.ds(pl.multiple_of(index * rows, rows), rows)
        there = pl.ds(pl.multiple_of(SIDE + index * rows, rows), rows)
        real = jnp.dot(first[here, :], signal[...], preferred_element_type=jnp.float32)
        imag = jnp.dot(first[there, :], signal[...], preferred_element_type=jnp.float32)
        cosine, sine = phase[0, here, :], phase[1, here, :]
        turned[here, :SIDE] = (real * cosine + imag * sine).astype(jnp.bfloat16)
        turned[here, SIDE:] = (imag * cosine - real * sine).astype(jnp.bfloat16)
        spectrum[here, :] = jnp.dot(
            turned[here, :], second[...], preferred_element_type=jnp.float32
        )
        return carry

    lax.fori_loop(0, SIDE // rows, chunk, 0)


def forward_received(received, other, mine, frame_slot, first, second, phase):
    rows = mine.shape[1]

    def body(*refs):
        received_refs, other_ref, mine_ref, slot_ref = refs[:ROUNDS], *refs[ROUNDS : ROUNDS + 3]
        first_ref, second_ref, phase_ref, spectrum, signal, turned = refs[ROUNDS + 3 :]
        segment = lax.axis_index("segment")
        core = lax.axis_index("template")
        following = jnp.minimum(segment + 1, slot_ref.shape[1] - 1)

        def place(source, frames):
            for part, half in enumerate((segment, following)):
                start = part * HALF + slot_ref[source, half] * rows
                signal[pl.ds(pl.multiple_of(start, rows), rows), :] = frames[part]

        for step in range(ROUNDS):
            place(segment ^ strain_mask(step, core), received_refs[step])
            place(segment ^ strain_mask(step, 1 - core), other_ref.at[step])
        place(segment, mine_ref)
        forward_body(signal, first_ref, second_ref, phase_ref, spectrum, turned)

    vmem = pl.BlockSpec(memory_space=pltpu.VMEM)
    return pl.pallas_call(
        body,
        out_shape=pltpu.VMEM((SIDE, SIDE), jnp.float32),
        in_specs=[vmem] * (ROUNDS + 2) + [pl.BlockSpec(memory_space=pltpu.SMEM)] + [vmem] * 3,
        out_specs=vmem,
        scratch_shapes=[
            pltpu.VMEM((SIDE, SIDE), jnp.bfloat16),
            pltpu.VMEM((SIDE, 2 * SIDE), jnp.bfloat16),
        ],
        compiler_params=pltpu.CompilerParams(vmem_limit_bytes=12 * MIB),
        cost_estimate=pl.CostEstimate(
            flops=4 * SIDE**3 * 2, bytes_accessed=6 * MIB, transcendentals=0
        ),
        name="forward",
    )(*received, other, mine, frame_slot, first, second, phase)


def forward_arranged(signal, first, second, phase):
    def body(signal_ref, first_ref, second_ref, phase_ref, spectrum, turned):
        forward_body(signal_ref, first_ref, second_ref, phase_ref, spectrum, turned)

    vmem = pl.BlockSpec(memory_space=pltpu.VMEM)
    return pl.pallas_call(
        body,
        out_shape=pltpu.VMEM((SIDE, SIDE), jnp.float32),
        in_specs=[vmem] * 4,
        out_specs=vmem,
        scratch_shapes=[pltpu.VMEM((SIDE, 2 * SIDE), jnp.bfloat16)],
        compiler_params=pltpu.CompilerParams(vmem_limit_bytes=12 * MIB),
        name="forward",
    )(signal, first, second, phase)


def owners_of(segment, core, doubled):
    if not doubled:
        return [[0]]
    near, far = 2 - core, 1 + core
    masks = [[0, 4], [near, near ^ 4], [far, far ^ 4, far ^ near, far ^ near ^ 4]]
    return [[segment ^ mask for mask in block] for block in masks]


def inverse(spectrum, blocks, edges, third, fourth, phase, doubled):
    n_blocks = len(blocks)
    shard = blocks[0].shape[2]
    quarter = HALF // 2
    wide = SIDE // 2

    def body(*refs):
        spectrum_ref, block_refs = refs[0], refs[1 : 1 + n_blocks]
        edge_ref, third_ref, fourth_ref, phase_ref = refs[1 + n_blocks : 5 + n_blocks]
        snr_ref, chisq_ref, peak_ref = refs[5 + n_blocks : 8 + n_blocks]
        gathered, flipped, masked, turned, sums, series = refs[8 + n_blocks :]
        segment = lax.axis_index("segment")
        core = lax.axis_index("template")
        for block, owners in zip(block_refs, owners_of(segment, core, doubled), strict=True):
            for place, owner in enumerate(owners):
                here = pl.ds(pl.multiple_of(owner * shard, shard), shard)
                for part in range(2):
                    gathered[part, here, :] = block[place, part]
        for part in range(2):
            flipped[:, part * HALF : (part + 1) * HALF] = gathered[part].T
        edge = [edge_ref[0, number] for number in range(3)]
        sums[...] = jnp.zeros_like(sums)
        step = 32

        def correlate(index, carry):
            here = pl.ds(pl.multiple_of(index * step, step), step)
            spec_real = [spectrum_ref[here, q * quarter : (q + 1) * quarter] for q in range(2)]
            spec_imag = [spectrum_ref[here, (q + 2) * quarter : (q + 3) * quarter] for q in range(2)]
            temp_real = [
                flipped[here, q * quarter : (q + 1) * quarter].astype(jnp.float32) for q in range(2)
            ]
            temp_imag = [
                flipped[here, (q + 2) * quarter : (q + 3) * quarter].astype(jnp.float32)
                for q in range(2)
            ]
            lane = lax.broadcasted_iota(jnp.int32, (step, quarter), 1)
            base = lane * SIDE + lax.broadcasted_iota(jnp.int32, (step, quarter), 0) + index * step
            zero = jnp.zeros((step, quarter), jnp.float32)
            corr, above, power = [], [], []
            for q in range(2):
                corr.append(
                    (
                        spec_real[q] * temp_real[q] + spec_imag[q] * temp_imag[q],
                        spec_imag[q] * temp_real[q] - spec_real[q] * temp_imag[q],
                    )
                )
                power.append(temp_real[q] * temp_real[q] + temp_imag[q] * temp_imag[q])
                bins = base + q * quarter * SIDE
                above.append([bins >= edge[number] for number in range(3)])
            inside = [
                [~above[0][0], None],
                [above[0][0] & ~above[0][1], ~above[1][1]],
                [above[0][1] & ~above[0][2], above[1][1] & ~above[1][2]],
                [None, above[1][2]],
            ]
            inside[1][1] = ~above[1][1] & above[1][0]
            for number in range(4):
                first_half, second_half = inside[number]
                if second_half is None:
                    chosen = [jnp.where(first_half, corr[0][part], zero) for part in range(2)]
                    strength = jnp.where(first_half, power[0], zero)
                elif first_half is None:
                    chosen = [jnp.where(second_half, corr[1][part], zero) for part in range(2)]
                    strength = jnp.where(second_half, power[1], zero)
                else:
                    chosen = [
                        jnp.where(
                            first_half, corr[0][part], jnp.where(second_half, corr[1][part], zero)
                        )
                        for part in range(2)
                    ]
                    strength = jnp.where(first_half, power[0], zero) + jnp.where(
                        second_half, power[1], zero
                    )
                for part in range(2):
                    masked[number, here, part * quarter : (part + 1) * quarter] = chosen[
                        part
                    ].astype(jnp.bfloat16)
                folded = strength[0:8]
                for start in range(8, step, 8):
                    folded = folded + strength[start : start + 8]
                sums[number] += folded
            return carry

        lax.fori_loop(0, SIDE // step, correlate, 0)

        def first_pass(number, carry):
            for tile in range(SIDE // wide):
                here = slice(tile * wide, (tile + 1) * wide)
                there = slice(SIDE + tile * wide, SIDE + (tile + 1) * wide)
                real = jnp.dot(
                    masked[number], third_ref[number, :, here], preferred_element_type=jnp.float32
                )
                imag = jnp.dot(
                    masked[number], third_ref[number, :, there], preferred_element_type=jnp.float32
                )
                cosine, sine = phase_ref[0, :, here], phase_ref[1, :, here]
                new_real = real * cosine - imag * sine
                new_imag = real * sine + imag * cosine
                for part, value in enumerate((new_real, new_imag)):
                    rows = slice(part * HALF, (part + 1) * HALF)
                    upper, lower = value[:HALF], value[HALF:]
                    turned[number, 0, rows, here] = (upper + lower).astype(jnp.bfloat16)
                    turned[number, 1, rows, here] = (upper - lower).astype(jnp.bfloat16)
            return carry

        lax.fori_loop(0, 4, first_pass, 0, unroll=True)

        bin_power = [jnp.sum(sums[number]) for number in range(4)]
        total = (bin_power[0] + bin_power[1]) + (bin_power[2] + bin_power[3])
        total_row = jnp.full((1, wide), total, jnp.float32)
        shares = [jnp.full((1, wide), bin_power[number], jnp.float32) / total_row for number in range(4)]
        scale = (1.0 / LENGTH) / total_row

        def second_pass(index, parity):
            columns = slice(index * wide, (index + 1) * wide)
            return [
                jnp.dot(
                    fourth_ref[parity],
                    turned[number, parity, :, columns],
                    preferred_element_type=jnp.float32,
                )
                for number in range(4)
            ]

        def finish(index, parity, pieces):
            real = [piece[:quarter] for piece in pieces]
            imag = [piece[quarter:] for piece in pieces]
            sum_real = (real[0] + real[1]) + (real[2] + real[3])
            sum_imag = (imag[0] + imag[1]) + (imag[2] + imag[3])
            snr = jnp.sqrt((sum_real * sum_real + sum_imag * sum_imag) * scale)
            chisq = None
            for number in range(4):
                diff_real = real[number] - shares[number] * sum_real
                diff_imag = imag[number] - shares[number] * sum_imag
                term = diff_real * diff_real + diff_imag * diff_imag
                chisq = term if chisq is None else chisq + term
            chisq = chisq * scale
            reduced = chisq * (1.0 / 6.0)
            inner = 0.5 + 0.5 * (reduced * reduced * reduced)
            weighted = snr * jnp.exp2(jnp.log2(inner) * (-1.0 / 6.0))
            newsnr = jnp.where(reduced > 1.0, weighted, snr)
            for tile in range(wide // 128):
                lanes = slice(tile * 128, (tile + 1) * 128)
                start = parity * (SIDE // 128) + index * (wide // 128) + tile
                rows = pl.ds(start, quarter, stride=2 * SIDE // 128)
                series[0, rows, :] = snr[:, lanes]
                series[1, rows, :] = chisq[:, lanes]
            return jnp.max(newsnr, axis=0, keepdims=True)

        peak = jnp.zeros((1, wide), jnp.float32)
        steps = [(index, parity) for index in range(SIDE // wide) for parity in range(2)]
        pieces = second_pass(*steps[0])
        for place, step in enumerate(steps):
            ahead = second_pass(*steps[place + 1]) if place + 1 < len(steps) else None
            peak = jnp.maximum(peak, finish(*step, pieces))
            pieces = ahead
        for kind, out_ref in enumerate((snr_ref, chisq_ref)):
            out_ref[0] = series[kind].reshape(1, LENGTH // 2).astype(jnp.bfloat16)
        peak_ref[...] = jnp.max(peak, axis=1, keepdims=True)

    vmem = pl.BlockSpec(memory_space=pltpu.VMEM)
    return pl.pallas_call(
        body,
        out_shape=(
            jax.ShapeDtypeStruct((1, 1, LENGTH // 2), jnp.bfloat16),
            jax.ShapeDtypeStruct((1, 1, LENGTH // 2), jnp.bfloat16),
            jax.ShapeDtypeStruct((1, 1), jnp.float32),
        ),
        in_specs=[vmem] * (1 + n_blocks) + [pl.BlockSpec(memory_space=pltpu.SMEM)] + [vmem] * 3,
        out_specs=(vmem, vmem, vmem),
        scratch_shapes=[
            pltpu.VMEM((2, HALF, SIDE), jnp.bfloat16),
            pltpu.VMEM((SIDE, SIDE), jnp.bfloat16),
            pltpu.VMEM((4, SIDE, HALF), jnp.bfloat16),
            pltpu.VMEM((4, 2, SIDE, SIDE), jnp.bfloat16),
            pltpu.VMEM((4, 8, quarter), jnp.float32),
            pltpu.VMEM((2, LENGTH // 256, 128), jnp.float32),
        ],
        compiler_params=pltpu.CompilerParams(vmem_limit_bytes=20 * MIB),
        name="inverse",
    )(spectrum, *blocks, edges, third, fourth, phase)


def exchange(value, mesh_shape, mask_of):
    groups, segments, cores = (mesh_shape[name] for name in AXES)
    pairs = []
    for group in range(groups):
        for segment in range(segments):
            for core in range(cores):
                if mask_of(core):
                    here = (group * segments + segment) * cores + core
                    other = segment ^ mask_of(core)
                    pairs.append((here, (group * segments + other) * cores + core))
    return lax.ppermute(value, AXES, pairs)


def arrange_plain(strain_frames, frame_slot):
    count = lax.axis_size("segment")
    position = lax.axis_index("segment")
    frame_length = strain_frames.shape[1]
    counter = jnp.arange(count, dtype=jnp.int32)
    slot_now = lax.dynamic_slice_in_dim(frame_slot, position, 1, 1)[:, 0]
    next_index = jnp.minimum(position + 1, count - 1)
    slot_next = lax.dynamic_slice_in_dim(frame_slot, next_index, 1, 1)[:, 0]

    def arrange(slots, frames):
        selector = (counter[:, None] == slots[None, :]).astype(jnp.bfloat16)
        placed = jnp.dot(selector, frames, preferred_element_type=jnp.float32)
        return placed.astype(jnp.bfloat16).reshape(HALF, SIDE)

    following_rows = jnp.concatenate(
        [strain_frames[1:], jnp.zeros((1, frame_length), jnp.bfloat16)], axis=0
    )
    outgoing = jnp.stack([strain_frames, following_rows], axis=1)
    received = lax.all_to_all(outgoing, "segment", split_axis=0, concat_axis=0, tiled=True)
    leading = arrange(slot_now, received[:, 0])
    trailing = arrange(slot_next, received[:, 1])
    return jnp.concatenate([leading, trailing])


def local(mesh_shape, strain_frames, frame_slot, templates, bin_edges):
    constants = tables()
    count = mesh_shape["segment"]
    rows = strain_frames.shape[1] // SIDE
    staged = count == 8 and mesh_shape["template"] == 2 and rows % 16 == 0
    if staged:
        across = exchange(templates, mesh_shape, lambda core: 4)
        *outgoing, mine, unpacked = split_frames(strain_frames, templates)
        pair = pair_shards(unpacked, across)
        *late, pair = lax.optimization_barrier((*outgoing[2:], pair))
        received = [
            exchange(value, mesh_shape, functools.partial(strain_mask, step))
            for step, value in enumerate([*outgoing[:2], *late])
        ]
        near = exchange(pair, mesh_shape, lambda core: 2 - core)
        first, second, third, fourth, phase = load_tables(constants, pair)
        other = lax.ppermute(jnp.stack(received), "template", [(0, 1), (1, 0)])
        far = exchange(jnp.concatenate([pair, near]), mesh_shape, lambda core: 1 + core)
        blocks = [pair, near, far]
        spectrum = forward_received(received, other, mine, frame_slot, first, second, phase)
    else:
        first, second, third, fourth, phase = constants
        signal = arrange_plain(strain_frames, frame_slot)
        whole = lax.all_gather(templates, "segment", axis=2, tiled=True)
        blocks = [whole.reshape(1, 2, HALF, SIDE)]
        spectrum = forward_arranged(signal, first, second, phase)
    return inverse(spectrum, blocks, bin_edges, third, fourth, phase, staged)


def solution(mesh):
    mesh_shape = dict(mesh.shape)

    def step(strain_frames, frame_slot, templates, bin_edges):
        return local(mesh_shape, strain_frames, frame_slot, templates, bin_edges)

    in_specs = (
        P("segment", None),
        P(),
        P(("groups", "template"), None, "segment"),
        P(("groups", "template"), None),
    )
    out_specs = (
        P("segment", ("groups", "template"), None),
        P("segment", ("groups", "template"), None),
        P("segment", ("groups", "template")),
    )
    return jax.shard_map(step, mesh=mesh, in_specs=in_specs, out_specs=out_specs, check_vma=False)
```

```python
import functools
import math

import jax
import jax.numpy as jnp
import ml_dtypes
import numpy as np
from jax import lax
from jax.experimental import pallas as pl
from jax.experimental.pallas import tpu as pltpu
from jax.sharding import PartitionSpec as P

SIDE = 512
HALF = SIDE // 2
LENGTH = SIDE * SIDE
AXES = ("groups", "segment", "template")
MIB = 1 << 20
STEP = 16
BIN_LOW = (0, 32, 96, 128)
ROUNDS = 4
MASKS = ((3, 2, 1, 0), (7, 6, 5, 4))


def strain_mask(step, core):
    if isinstance(core, int):
        return MASKS[core][step]
    return jnp.where(core == 0, MASKS[0][step], MASKS[1][step])


def turn(rows, columns, modulus):
    product = np.outer(rows, columns) % modulus
    angles = 2.0 * math.pi / modulus * product.astype(np.float64)
    return np.cos(angles), np.sin(angles)


def tables():
    digit = np.arange(SIDE)
    cosine, sine = turn(digit, digit, SIDE)
    first = np.concatenate([cosine, -sine], axis=0)
    low = slice(0, HALF)
    second = np.block([[cosine[:, low], -sine[:, low]], [sine[:, low], cosine[:, low]]])
    third = []
    column = np.arange(HALF // 2)
    for start in BIN_LOW:
        chosen = np.where(column >= start, column, column + HALF // 2)
        third.append(
            np.block([[cosine[chosen], sine[chosen]], [-sine[chosen], cosine[chosen]]])
        )
    fourth = []
    for parity in range(2):
        kept = slice(HALF // 2 + parity, HALF // 2 + HALF, 2)
        fourth.append(
            np.block(
                [[cosine[kept, low], -sine[kept, low]], [sine[kept, low], cosine[kept, low]]]
            )
        )
    phase_cos, phase_sin = turn(digit, digit, LENGTH)
    phase = np.stack([phase_cos, phase_sin]).astype(np.float32)
    coarse = [x[::STEP] for x in (phase_cos, phase_sin)]
    fine = [x[:STEP] for x in (phase_cos, phase_sin)]
    factors = np.concatenate([*coarse, *fine]).astype(np.float32)


    narrow = [x.astype(np.float32).astype(ml_dtypes.bfloat16) for x in (first, second, np.stack(third), np.stack(fourth))]
    return (*narrow, phase, factors)


def in_hbm(*arrays):
    return [pltpu.with_memory_space_constraint(x, pltpu.HBM) for x in arrays]


def in_vmem(*arrays):
    return [pltpu.with_memory_space_constraint(x, pltpu.VMEM) for x in arrays]


def spread(source, wide, count, rows):
    tiles = SIDE // 128
    for row in range(rows):
        for tile in range(tiles):
            place = (row * tiles + tile) * 128
            wide[tile, pl.ds(row, count, stride=rows), :] = source[:, place : place + 128].astype(
                jnp.float32
            )


def split_frames(frames, shard):
    count, samples = frames.shape
    rows = samples // SIDE
    tiles = SIDE // 128

    def body(frames_hbm, shard_hbm, *refs):
        outs, (unpacked, wide, narrow, frames_ref, shard_ref, arrived) = (
            refs[: ROUNDS + 1],
            refs[ROUNDS + 1 :],
        )
        copies = [
            pltpu.make_async_copy(frames_hbm, frames_ref, arrived.at[0]),
            pltpu.make_async_copy(shard_hbm, shard_ref, arrived.at[1]),
        ]
        for copy in copies:
            copy.start()
        segment = lax.axis_index("segment")
        core = lax.axis_index("template")
        wide[:, count * rows :, :] = jnp.zeros((tiles, rows, 128), jnp.float32)
        copies[0].wait()
        spread(frames_ref, wide, count, rows)
        for step, out_ref in enumerate(outs):
            mask = strain_mask(step, core) if step < ROUNDS else 0
            start = pl.multiple_of((segment ^ mask) * rows, rows)
            for tile in range(tiles):
                out_ref[:, :, tile * 128 : tile * 128 + 128] = (
                    wide[tile, pl.ds(start, 2 * rows), :].astype(jnp.bfloat16).reshape(2, rows, 128)
                )
        copies[1].wait()
        unpack(shard_ref, narrow, unpacked.at[0])

    vmem = pl.BlockSpec(memory_space=pltpu.VMEM)
    return pl.pallas_call(
        body,
        out_shape=[pltpu.VMEM((2, rows, SIDE), jnp.bfloat16)] * (ROUNDS + 1)
        + [pltpu.VMEM((1, 2, rows, SIDE), jnp.bfloat16)],
        in_specs=[pl.BlockSpec(memory_space=pl.ANY)] * 2,
        out_specs=[vmem] * (ROUNDS + 2),
        scratch_shapes=[
            pltpu.VMEM((tiles, (count + 1) * rows, 128), jnp.float32),
            pltpu.VMEM((tiles, 2 * rows, 128), jnp.float32),
            pltpu.VMEM(frames.shape, frames.dtype),
            pltpu.VMEM(shard.shape, shard.dtype),
            pltpu.SemaphoreType.DMA((2,)),
        ],
        compiler_params=pltpu.CompilerParams(vmem_limit_bytes=4 * MIB),
        name="split_frames",
    )(*in_hbm(frames, shard))


def unpack(shard_ref, narrow, out_ref):
    rows = out_ref.shape[1]
    spread(shard_ref.at[0], narrow, 2, rows)
    for tile in range(SIDE // 128):
        out_ref[:, :, tile * 128 : tile * 128 + 128] = (
            narrow[tile].astype(jnp.bfloat16).reshape(2, rows, 128)
        )


def pair_shards(unpacked, across):
    rows = unpacked.shape[2]

    def body(unpacked_ref, across_ref, out_ref, narrow):
        out_ref[0] = unpacked_ref[0]
        unpack(across_ref, narrow, out_ref.at[1])

    vmem = pl.BlockSpec(memory_space=pltpu.VMEM)
    return pl.pallas_call(
        body,
        out_shape=pltpu.VMEM((2, 2, rows, SIDE), jnp.bfloat16),
        in_specs=[vmem, vmem],
        out_specs=vmem,
        scratch_shapes=[pltpu.VMEM((SIDE // 128, 2 * rows, 128), jnp.float32)],
        compiler_params=pltpu.CompilerParams(vmem_limit_bytes=4 * MIB),
        name="pair_shards",
    )(unpacked, across)


def load_tables(arrays, after):
    count = len(arrays)

    def body(*refs):
        sources, outs, arrived = refs[:count], refs[count + 1 : 2 * count + 1], refs[-1]
        copies = [
            pltpu.make_async_copy(source, out, arrived.at[place])
            for place, (source, out) in enumerate(zip(sources, outs, strict=True))
        ]
        for copy in copies:
            copy.start()
        for copy in copies:
            copy.wait()

    hbm = pl.BlockSpec(memory_space=pl.ANY)
    return pl.pallas_call(
        body,
        out_shape=[pltpu.VMEM(x.shape, x.dtype) for x in arrays],
        in_specs=[hbm] * (count + 1),
        out_specs=[pl.BlockSpec(memory_space=pltpu.VMEM)] * count,
        scratch_shapes=[pltpu.SemaphoreType.DMA((count,))],
        compiler_params=pltpu.CompilerParams(vmem_limit_bytes=1 * MIB),
        cost_estimate=pl.CostEstimate(flops=0, bytes_accessed=4 * MIB, transcendentals=0),
        name="load_tables",
    )(*in_hbm(*arrays), after)


def phases(factors, first, count):
    groups = SIDE // STEP
    coarse_cos, coarse_sin = (
        factors[pl.ds(kind * groups + first, count), :][:, None, :] for kind in range(2)
    )
    fine_cos, fine_sin = (
        factors[2 * groups + kind * STEP : 2 * groups + (kind + 1) * STEP, :][None]
        for kind in range(2)
    )
    cosine = coarse_cos * fine_cos - coarse_sin * fine_sin
    sine = coarse_sin * fine_cos + coarse_cos * fine_sin
    return cosine.reshape(count * STEP, SIDE), sine.reshape(count * STEP, SIDE)


def forward_body(signal, first, second, factors, spectrum, turned):
    rows = SIDE // 2

    def chunk(index):
        here = pl.ds(index * rows, rows)
        there = pl.ds(SIDE + index * rows, rows)
        real = jnp.dot(first[here, :], signal[...], preferred_element_type=jnp.float32)
        imag = jnp.dot(first[there, :], signal[...], preferred_element_type=jnp.float32)
        cosine, sine = phases(factors, index * (rows // STEP), rows // STEP)
        turned[here, :SIDE] = (real * cosine + imag * sine).astype(jnp.bfloat16)
        turned[here, SIDE:] = (imag * cosine - real * sine).astype(jnp.bfloat16)
        spectrum[here, :] = jnp.dot(
            turned[here, :], second[...], preferred_element_type=jnp.float32
        )

    for index in range(SIDE // rows):
        chunk(index)


def forward_received(received, other, mine, frame_slot, first, second, factors):
    rows = mine.shape[1]

    def body(*refs):
        received_refs, other_ref, mine_ref, slot_ref = refs[:ROUNDS], *refs[ROUNDS : ROUNDS + 3]
        first_ref, second_ref, phase_ref, spectrum, signal, turned = refs[ROUNDS + 3 :]
        segment = lax.axis_index("segment")
        core = lax.axis_index("template")
        following = jnp.minimum(segment + 1, slot_ref.shape[1] - 1)

        def place(source, frames):
            for part, half in enumerate((segment, following)):
                start = part * HALF + slot_ref[source, half] * rows
                signal[pl.ds(pl.multiple_of(start, rows), rows), :] = frames[part]

        for step in range(ROUNDS):
            place(segment ^ strain_mask(step, core), received_refs[step])
            place(segment ^ strain_mask(step, 1 - core), other_ref.at[step])
        place(segment, mine_ref)
        forward_body(signal, first_ref, second_ref, phase_ref, spectrum, turned)

    vmem = pl.BlockSpec(memory_space=pltpu.VMEM)
    return pl.pallas_call(
        body,
        out_shape=pltpu.VMEM((SIDE, SIDE), jnp.float32),
        in_specs=[vmem] * (ROUNDS + 2) + [pl.BlockSpec(memory_space=pltpu.SMEM)] + [vmem] * 3,
        out_specs=vmem,
        scratch_shapes=[
            pltpu.VMEM((SIDE, SIDE), jnp.bfloat16),
            pltpu.VMEM((SIDE, 2 * SIDE), jnp.bfloat16),
        ],
        compiler_params=pltpu.CompilerParams(vmem_limit_bytes=12 * MIB),
        cost_estimate=pl.CostEstimate(
            flops=4 * SIDE**3 * 2, bytes_accessed=6 * MIB, transcendentals=0
        ),
        name="forward",
    )(*received, other, mine, frame_slot, first, *in_vmem(second), factors)


def forward_arranged(signal, first, second, factors):
    def body(signal_ref, first_ref, second_ref, phase_ref, spectrum, turned):
        forward_body(signal_ref, first_ref, second_ref, phase_ref, spectrum, turned)

    vmem = pl.BlockSpec(memory_space=pltpu.VMEM)
    return pl.pallas_call(
        body,
        out_shape=pltpu.VMEM((SIDE, SIDE), jnp.float32),
        in_specs=[vmem] * 4,
        out_specs=vmem,
        scratch_shapes=[pltpu.VMEM((SIDE, 2 * SIDE), jnp.bfloat16)],
        compiler_params=pltpu.CompilerParams(vmem_limit_bytes=12 * MIB),
        name="forward",
    )(signal, first, second, factors)


def owners_of(segment, core, doubled):
    if not doubled:
        return [[0]]
    near, far = 2 - core, 1 + core
    masks = [[0, 4], [near, near ^ 4], [far, far ^ 4, far ^ near, far ^ near ^ 4]]
    return [[segment ^ mask for mask in block] for block in masks]


def inverse(spectrum, blocks, edges, third, fourth, phase, doubled):
    n_blocks = len(blocks)
    shard = blocks[0].shape[2]
    quarter = HALF // 2
    wide = SIDE // 2

    def body(*refs):
        spectrum_ref, block_refs = refs[0], refs[1 : 1 + n_blocks]
        edge_ref, third_ref, fourth_ref, phase_ref = refs[1 + n_blocks : 5 + n_blocks]
        snr_ref, chisq_ref, peak_ref = refs[5 + n_blocks : 8 + n_blocks]
        gathered, flipped, masked, turned, sums, series = refs[8 + n_blocks :]
        segment = lax.axis_index("segment")
        core = lax.axis_index("template")
        for block, owners in zip(block_refs, owners_of(segment, core, doubled), strict=True):
            for place, owner in enumerate(owners):
                here = pl.ds(pl.multiple_of(owner * shard, shard), shard)
                for part in range(2):
                    gathered[part, here, :] = block[place, part]
        for part in range(2):
            flipped[:, part * HALF : (part + 1) * HALF] = gathered[part].T
        edge = [edge_ref[0, number] for number in range(3)]
        sums[...] = jnp.zeros_like(sums)
        step = 32

        def correlate(index, carry):
            here = pl.ds(pl.multiple_of(index * step, step), step)
            spec_real = [spectrum_ref[here, q * quarter : (q + 1) * quarter] for q in range(2)]
            spec_imag = [spectrum_ref[here, (q + 2) * quarter : (q + 3) * quarter] for q in range(2)]
            temp_real = [
                flipped[here, q * quarter : (q + 1) * quarter].astype(jnp.float32) for q in range(2)
            ]
            temp_imag = [
                flipped[here, (q + 2) * quarter : (q + 3) * quarter].astype(jnp.float32)
                for q in range(2)
            ]
            lane = lax.broadcasted_iota(jnp.int32, (step, quarter), 1)
            base = lane * SIDE + lax.broadcasted_iota(jnp.int32, (step, quarter), 0) + index * step
            zero = jnp.zeros((step, quarter), jnp.float32)
            corr, above, power = [], [], []
            for q in range(2):
                corr.append(
                    (
                        spec_real[q] * temp_real[q] + spec_imag[q] * temp_imag[q],
                        spec_imag[q] * temp_real[q] - spec_real[q] * temp_imag[q],
                    )
                )
                power.append(temp_real[q] * temp_real[q] + temp_imag[q] * temp_imag[q])
                bins = base + q * quarter * SIDE
                above.append([bins >= edge[number] for number in range(3)])
            inside = [
                [~above[0][0], None],
                [above[0][0] & ~above[0][1], ~above[1][1]],
                [above[0][1] & ~above[0][2], above[1][1] & ~above[1][2]],
                [None, above[1][2]],
            ]
            inside[1][1] = ~above[1][1] & above[1][0]
            for number in range(4):
                first_half, second_half = inside[number]
                if second_half is None:
                    chosen = [jnp.where(first_half, corr[0][part], zero) for part in range(2)]
                    strength = jnp.where(first_half, power[0], zero)
                elif first_half is None:
                    chosen = [jnp.where(second_half, corr[1][part], zero) for part in range(2)]
                    strength = jnp.where(second_half, power[1], zero)
                else:
                    chosen = [
                        jnp.where(
                            first_half, corr[0][part], jnp.where(second_half, corr[1][part], zero)
                        )
                        for part in range(2)
                    ]
                    strength = jnp.where(first_half, power[0], zero) + jnp.where(
                        second_half, power[1], zero
                    )
                for part in range(2):
                    masked[number, here, part * quarter : (part + 1) * quarter] = chosen[
                        part
                    ].astype(jnp.bfloat16)
                folded = strength[0:8]
                for start in range(8, step, 8):
                    folded = folded + strength[start : start + 8]
                sums[number] += folded
            return carry

        lax.fori_loop(0, SIDE // step, correlate, 0)

        def first_pass(number, carry):
            for tile in range(SIDE // wide):
                here = slice(tile * wide, (tile + 1) * wide)
                there = slice(SIDE + tile * wide, SIDE + (tile + 1) * wide)
                real = jnp.dot(
                    masked[number], third_ref[number, :, here], preferred_element_type=jnp.float32
                )
                imag = jnp.dot(
                    masked[number], third_ref[number, :, there], preferred_element_type=jnp.float32
                )
                cosine, sine = phase_ref[0, :, here], phase_ref[1, :, here]
                new_real = real * cosine - imag * sine
                new_imag = real * sine + imag * cosine
                for part, value in enumerate((new_real, new_imag)):
                    rows = slice(part * HALF, (part + 1) * HALF)
                    upper, lower = value[:HALF], value[HALF:]
                    turned[number, 0, rows, here] = (upper + lower).astype(jnp.bfloat16)
                    turned[number, 1, rows, here] = (upper - lower).astype(jnp.bfloat16)
            return carry

        lax.fori_loop(0, 4, first_pass, 0, unroll=True)

        bin_power = [jnp.sum(sums[number]) for number in range(4)]
        total = (bin_power[0] + bin_power[1]) + (bin_power[2] + bin_power[3])
        total_row = jnp.full((1, wide), total, jnp.float32)
        shares = [jnp.full((1, wide), bin_power[number], jnp.float32) / total_row for number in range(4)]
        scale = (1.0 / LENGTH) / total_row

        def second_pass(index, parity):
            columns = slice(index * wide, (index + 1) * wide)
            return [
                jnp.dot(
                    fourth_ref[parity],
                    turned[number, parity, :, columns],
                    preferred_element_type=jnp.float32,
                )
                for number in range(4)
            ]

        def finish(index, parity, pieces):
            real = [piece[:quarter] for piece in pieces]
            imag = [piece[quarter:] for piece in pieces]
            sum_real = (real[0] + real[1]) + (real[2] + real[3])
            sum_imag = (imag[0] + imag[1]) + (imag[2] + imag[3])
            snr = jnp.sqrt((sum_real * sum_real + sum_imag * sum_imag) * scale)
            chisq = None
            for number in range(4):
                diff_real = real[number] - shares[number] * sum_real
                diff_imag = imag[number] - shares[number] * sum_imag
                term = diff_real * diff_real + diff_imag * diff_imag
                chisq = term if chisq is None else chisq + term
            chisq = chisq * scale
            reduced = chisq * (1.0 / 6.0)
            inner = 0.5 + 0.5 * (reduced * reduced * reduced)
            weighted = snr * jnp.exp2(jnp.log2(inner) * (-1.0 / 6.0))
            newsnr = jnp.where(reduced > 1.0, weighted, snr)
            for tile in range(wide // 128):
                lanes = slice(tile * 128, (tile + 1) * 128)
                start = parity * (SIDE // 128) + index * (wide // 128) + tile
                rows = pl.ds(start, quarter, stride=2 * SIDE // 128)
                series[0, rows, :] = snr[:, lanes]
                series[1, rows, :] = chisq[:, lanes]
            return jnp.max(newsnr, axis=0, keepdims=True)

        peak = jnp.zeros((1, wide), jnp.float32)
        steps = [(index, parity) for index in range(SIDE // wide) for parity in range(2)]
        pieces = second_pass(*steps[0])
        for place, step in enumerate(steps):
            ahead = second_pass(*steps[place + 1]) if place + 1 < len(steps) else None
            peak = jnp.maximum(peak, finish(*step, pieces))
            pieces = ahead
        for kind, out_ref in enumerate((snr_ref, chisq_ref)):
            out_ref[0] = series[kind].reshape(1, LENGTH // 2).astype(jnp.bfloat16)
        peak_ref[...] = jnp.max(peak, axis=1, keepdims=True)

    vmem = pl.BlockSpec(memory_space=pltpu.VMEM)
    return pl.pallas_call(
        body,
        out_shape=(
            jax.ShapeDtypeStruct((1, 1, LENGTH // 2), jnp.bfloat16),
            jax.ShapeDtypeStruct((1, 1, LENGTH // 2), jnp.bfloat16),
            jax.ShapeDtypeStruct((1, 1), jnp.float32),
        ),
        in_specs=[vmem] * (1 + n_blocks) + [pl.BlockSpec(memory_space=pltpu.SMEM)] + [vmem] * 3,
        out_specs=(vmem, vmem, vmem),
        scratch_shapes=[
            pltpu.VMEM((2, HALF, SIDE), jnp.bfloat16),
            pltpu.VMEM((SIDE, SIDE), jnp.bfloat16),
            pltpu.VMEM((4, SIDE, HALF), jnp.bfloat16),
            pltpu.VMEM((4, 2, SIDE, SIDE), jnp.bfloat16),
            pltpu.VMEM((4, 8, quarter), jnp.float32),
            pltpu.VMEM((2, LENGTH // 256, 128), jnp.float32),
        ],
        compiler_params=pltpu.CompilerParams(vmem_limit_bytes=16 * MIB),
        name="inverse",
    )(spectrum, *blocks, edges, *in_vmem(third, fourth, phase))


def exchange(value, mesh_shape, mask_of):
    groups, segments, cores = (mesh_shape[name] for name in AXES)
    pairs = []
    for group in range(groups):
        for segment in range(segments):
            for core in range(cores):
                if mask_of(core):
                    here = (group * segments + segment) * cores + core
                    other = segment ^ mask_of(core)
                    pairs.append((here, (group * segments + other) * cores + core))
    return lax.ppermute(value, AXES, pairs)


def arrange_plain(strain_frames, frame_slot):
    count = lax.axis_size("segment")
    position = lax.axis_index("segment")
    frame_length = strain_frames.shape[1]
    counter = jnp.arange(count, dtype=jnp.int32)
    slot_now = lax.dynamic_slice_in_dim(frame_slot, position, 1, 1)[:, 0]
    next_index = jnp.minimum(position + 1, count - 1)
    slot_next = lax.dynamic_slice_in_dim(frame_slot, next_index, 1, 1)[:, 0]

    def arrange(slots, frames):
        selector = (counter[:, None] == slots[None, :]).astype(jnp.bfloat16)
        placed = jnp.dot(selector, frames, preferred_element_type=jnp.float32)
        return placed.astype(jnp.bfloat16).reshape(HALF, SIDE)

    following_rows = jnp.concatenate(
        [strain_frames[1:], jnp.zeros((1, frame_length), jnp.bfloat16)], axis=0
    )
    outgoing = jnp.stack([strain_frames, following_rows], axis=1)
    received = lax.all_to_all(outgoing, "segment", split_axis=0, concat_axis=0, tiled=True)
    leading = arrange(slot_now, received[:, 0])
    trailing = arrange(slot_next, received[:, 1])
    return jnp.concatenate([leading, trailing])


def local(mesh_shape, strain_frames, frame_slot, templates, bin_edges):
    constants = tables()
    count = mesh_shape["segment"]
    rows = strain_frames.shape[1] // SIDE
    staged = count == 8 and mesh_shape["template"] == 2 and rows % 16 == 0
    if staged:
        across = exchange(templates, mesh_shape, lambda core: 4)
        *outgoing, mine, unpacked = split_frames(strain_frames, templates)
        received = [
            exchange(value, mesh_shape, functools.partial(strain_mask, step))
            for step, value in enumerate(outgoing[:3])
        ]
        pair = pair_shards(unpacked, across)
        *late, pair = lax.optimization_barrier((*outgoing[3:], pair))
        received += [
            exchange(value, mesh_shape, functools.partial(strain_mask, step + 3))
            for step, value in enumerate(late)
        ]
        near = exchange(pair, mesh_shape, lambda core: 2 - core)
        first, second, third, fourth, phase, factors = constants
        first, factors = load_tables((first, factors), pair)
        *received, first = lax.optimization_barrier((*received, first))
        other = lax.ppermute(jnp.stack(received), "template", [(0, 1), (1, 0)])
        far = exchange(jnp.concatenate([pair, near]), mesh_shape, lambda core: 1 + core)
        blocks = [pair, near, far]
        spectrum = forward_received(received, other, mine, frame_slot, first, second, factors)
    else:
        first, second, third, fourth, phase, factors = constants
        signal = arrange_plain(strain_frames, frame_slot)
        whole = lax.all_gather(templates, "segment", axis=2, tiled=True)
        blocks = [whole.reshape(1, 2, HALF, SIDE)]
        spectrum = forward_arranged(signal, first, second, factors)
    return inverse(spectrum, blocks, bin_edges, third, fourth, phase, staged)


def solution(mesh):
    mesh_shape = dict(mesh.shape)

    def step(strain_frames, frame_slot, templates, bin_edges):
        return local(mesh_shape, strain_frames, frame_slot, templates, bin_edges)

    in_specs = (
        P("segment", None),
        P(),
        P(("groups", "template"), None, "segment"),
        P(("groups", "template"), None),
    )
    out_specs = (
        P("segment", ("groups", "template"), None),
        P("segment", ("groups", "template"), None),
        P("segment", ("groups", "template")),
    )
    return jax.shard_map(step, mesh=mesh, in_specs=in_specs, out_specs=out_specs, check_vma=False)
```

```python
import functools
import math

import jax
import jax.numpy as jnp
import ml_dtypes
import numpy as np
from jax import lax
from jax.experimental import pallas as pl
from jax.experimental.pallas import tpu as pltpu
from jax.sharding import PartitionSpec as P

SIDE = 512
HALF = SIDE // 2
LENGTH = SIDE * SIDE
AXES = ("groups", "segment", "template")
MIB = 1 << 20
STEP = 16
BIN_LOW = (0, 32, 96, 128)
ROUNDS = 4
MASKS = ((7, 2, 1, 0), (3, 6, 5, 4))


def strain_mask(step, core):
    if isinstance(core, int):
        return MASKS[core][step]
    return jnp.where(core == 0, MASKS[0][step], MASKS[1][step])


def turn(rows, columns, modulus):
    product = np.outer(rows, columns) % modulus
    angles = 2.0 * math.pi / modulus * product.astype(np.float64)
    return np.cos(angles), np.sin(angles)


def tables():
    digit = np.arange(SIDE)
    cosine, sine = turn(digit, digit, SIDE)
    first = np.concatenate([cosine, -sine], axis=0)
    low = slice(0, HALF)
    second = np.block([[cosine[:, low], -sine[:, low]], [sine[:, low], cosine[:, low]]])
    third = []
    column = np.arange(HALF // 2)
    for start in BIN_LOW:
        chosen = np.where(column >= start, column, column + HALF // 2)
        real = np.concatenate([cosine[chosen], -sine[chosen]])
        imag = np.concatenate([sine[chosen], cosine[chosen]])
        tiles = np.stack([real, imag], axis=1).reshape(HALF, 2, SIDE // 128, 128)
        third.append(tiles.swapaxes(1, 2).reshape(HALF, 2 * SIDE))
    fourth = []
    for parity in range(2):
        kept = slice(HALF // 2 + parity, HALF // 2 + HALF, 2)
        real = np.concatenate([cosine[kept, low], -sine[kept, low]], axis=1)
        imag = np.concatenate([sine[kept, low], cosine[kept, low]], axis=1)
        pairs = np.stack([real.reshape(-1, 8, SIDE), imag.reshape(-1, 8, SIDE)], axis=1)
        fourth.append(pairs.reshape(HALF, SIDE))
    phase_cos, phase_sin = turn(digit, digit, LENGTH)
    phase = np.stack([phase_cos, phase_sin]).astype(np.float32).astype(ml_dtypes.bfloat16)
    coarse = [x[::STEP] for x in (phase_cos, phase_sin)]
    fine = [x[:STEP] for x in (phase_cos, phase_sin)]
    factors = np.concatenate([*coarse, *fine]).astype(np.float32)


    narrow = [x.astype(np.float32).astype(ml_dtypes.bfloat16) for x in (first, second, np.stack(third), np.stack(fourth))]
    return (*narrow, phase, factors)


def in_hbm(*arrays):
    return [pltpu.with_memory_space_constraint(x, pltpu.HBM) for x in arrays]


def in_vmem(*arrays):
    return [pltpu.with_memory_space_constraint(x, pltpu.VMEM) for x in arrays]


def spread(source, wide, count, rows):
    tiles = SIDE // 128
    for row in range(rows):
        for tile in range(tiles):
            place = (row * tiles + tile) * 128
            wide[tile, pl.ds(row, count, stride=rows), :] = source[:, place : place + 128].astype(
                jnp.float32
            )


def split_frames(frames, shard):
    count, samples = frames.shape
    rows = samples // SIDE
    tiles = SIDE // 128

    def body(frames_hbm, shard_hbm, *refs):
        outs, (unpacked, wide, narrow, frames_ref, shard_ref, arrived) = (
            refs[: ROUNDS + 1],
            refs[ROUNDS + 1 :],
        )
        copies = [
            pltpu.make_async_copy(frames_hbm, frames_ref, arrived.at[0]),
            pltpu.make_async_copy(shard_hbm, shard_ref, arrived.at[1]),
        ]
        for copy in copies:
            copy.start()
        segment = lax.axis_index("segment")
        core = lax.axis_index("template")
        wide[:, count * rows :, :] = jnp.zeros((tiles, rows, 128), jnp.float32)
        copies[0].wait()
        spread(frames_ref, wide, count, rows)
        for step, out_ref in enumerate(outs):
            mask = strain_mask(step, core) if step < ROUNDS else 0
            start = pl.multiple_of((segment ^ mask) * rows, rows)
            for tile in range(tiles):
                out_ref[:, :, tile * 128 : tile * 128 + 128] = (
                    wide[tile, pl.ds(start, 2 * rows), :].astype(jnp.bfloat16).reshape(2, rows, 128)
                )
        copies[1].wait()
        unpack(shard_ref, narrow, unpacked.at[0])

    vmem = pl.BlockSpec(memory_space=pltpu.VMEM)
    return pl.pallas_call(
        body,
        out_shape=[pltpu.VMEM((2, rows, SIDE), jnp.bfloat16)] * (ROUNDS + 1)
        + [pltpu.VMEM((1, 2, rows, SIDE), jnp.bfloat16)],
        in_specs=[pl.BlockSpec(memory_space=pl.ANY)] * 2,
        out_specs=[vmem] * (ROUNDS + 2),
        scratch_shapes=[
            pltpu.VMEM((tiles, (count + 1) * rows, 128), jnp.float32),
            pltpu.VMEM((tiles, 2 * rows, 128), jnp.float32),
            pltpu.VMEM(frames.shape, frames.dtype),
            pltpu.VMEM(shard.shape, shard.dtype),
            pltpu.SemaphoreType.DMA((2,)),
        ],
        compiler_params=pltpu.CompilerParams(vmem_limit_bytes=4 * MIB),
        name="split_frames",
    )(*in_hbm(frames, shard))


def unpack(shard_ref, narrow, out_ref):
    rows = out_ref.shape[1]
    spread(shard_ref.at[0], narrow, 2, rows)
    for tile in range(SIDE // 128):
        out_ref[:, :, tile * 128 : tile * 128 + 128] = (
            narrow[tile].astype(jnp.bfloat16).reshape(2, rows, 128)
        )


def pair_shards(unpacked, across):
    rows = unpacked.shape[2]

    def body(unpacked_ref, across_ref, out_ref, narrow):
        out_ref[0] = unpacked_ref[0]
        unpack(across_ref, narrow, out_ref.at[1])

    vmem = pl.BlockSpec(memory_space=pltpu.VMEM)
    return pl.pallas_call(
        body,
        out_shape=pltpu.VMEM((2, 2, rows, SIDE), jnp.bfloat16),
        in_specs=[vmem, vmem],
        out_specs=vmem,
        scratch_shapes=[pltpu.VMEM((SIDE // 128, 2 * rows, 128), jnp.float32)],
        compiler_params=pltpu.CompilerParams(vmem_limit_bytes=4 * MIB),
        name="pair_shards",
    )(unpacked, across)


def load_tables(arrays, after):
    count = len(arrays)

    def body(*refs):
        sources, outs, arrived = refs[:count], refs[count + 1 : 2 * count + 1], refs[-1]
        copies = [
            pltpu.make_async_copy(source, out, arrived.at[place])
            for place, (source, out) in enumerate(zip(sources, outs, strict=True))
        ]
        for copy in copies:
            copy.start()
        for copy in copies:
            copy.wait()

    hbm = pl.BlockSpec(memory_space=pl.ANY)
    return pl.pallas_call(
        body,
        out_shape=[pltpu.VMEM(x.shape, x.dtype) for x in arrays],
        in_specs=[hbm] * (count + 1),
        out_specs=[pl.BlockSpec(memory_space=pltpu.VMEM)] * count,
        scratch_shapes=[pltpu.SemaphoreType.DMA((count,))],
        compiler_params=pltpu.CompilerParams(vmem_limit_bytes=1 * MIB),
        cost_estimate=pl.CostEstimate(flops=0, bytes_accessed=4 * MIB, transcendentals=0),
        name="load_tables",
    )(*in_hbm(*arrays), after)


def phases(factors, first, count):
    groups = SIDE // STEP
    coarse_cos, coarse_sin = (
        factors[pl.ds(kind * groups + first, count), :][:, None, :] for kind in range(2)
    )
    fine_cos, fine_sin = (
        factors[2 * groups + kind * STEP : 2 * groups + (kind + 1) * STEP, :][None]
        for kind in range(2)
    )
    cosine = coarse_cos * fine_cos - coarse_sin * fine_sin
    sine = coarse_sin * fine_cos + coarse_cos * fine_sin
    return cosine.reshape(count * STEP, SIDE), sine.reshape(count * STEP, SIDE)


def forward_body(signal, first, second, factors, spectrum, turned):
    rows = SIDE // 2

    def chunk(index):
        here = pl.ds(index * rows, rows)
        there = pl.ds(SIDE + index * rows, rows)
        real = jnp.dot(first[here, :], signal[...], preferred_element_type=jnp.float32)
        imag = jnp.dot(first[there, :], signal[...], preferred_element_type=jnp.float32)
        cosine, sine = phases(factors, index * (rows // STEP), rows // STEP)
        turned[here, :SIDE] = (real * cosine + imag * sine).astype(jnp.bfloat16)
        turned[here, SIDE:] = (imag * cosine - real * sine).astype(jnp.bfloat16)
        spectrum[here, :] = jnp.dot(
            turned[here, :], second[...], preferred_element_type=jnp.float32
        )

    for index in range(SIDE // rows):
        chunk(index)


def forward_received(received, other, mine, frame_slot, first, second, factors):
    rows = mine.shape[1]

    def body(*refs):
        received_refs, other_ref, mine_ref, slot_ref = refs[:ROUNDS], *refs[ROUNDS : ROUNDS + 3]
        first_ref, second_ref, phase_ref, spectrum, signal, turned = refs[ROUNDS + 3 :]
        segment = lax.axis_index("segment")
        core = lax.axis_index("template")
        following = jnp.minimum(segment + 1, slot_ref.shape[1] - 1)

        def place(source, frames):
            for part, half in enumerate((segment, following)):
                start = part * HALF + slot_ref[source, half] * rows
                signal[pl.ds(pl.multiple_of(start, rows), rows), :] = frames[part]

        for step in range(ROUNDS):
            place(segment ^ strain_mask(step, core), received_refs[step])
            place(segment ^ strain_mask(step, 1 - core), other_ref.at[step])
        place(segment, mine_ref)
        forward_body(signal, first_ref, second_ref, phase_ref, spectrum, turned)

    vmem = pl.BlockSpec(memory_space=pltpu.VMEM)
    return pl.pallas_call(
        body,
        out_shape=pltpu.VMEM((SIDE, SIDE), jnp.float32),
        in_specs=[vmem] * (ROUNDS + 2) + [pl.BlockSpec(memory_space=pltpu.SMEM)] + [vmem] * 3,
        out_specs=vmem,
        scratch_shapes=[
            pltpu.VMEM((SIDE, SIDE), jnp.bfloat16),
            pltpu.VMEM((SIDE, 2 * SIDE), jnp.bfloat16),
        ],
        compiler_params=pltpu.CompilerParams(vmem_limit_bytes=12 * MIB),
        cost_estimate=pl.CostEstimate(
            flops=4 * SIDE**3 * 2, bytes_accessed=6 * MIB, transcendentals=0
        ),
        name="forward",
    )(*received, other, mine, frame_slot, first, *in_vmem(second), factors)


def forward_arranged(signal, first, second, factors):
    def body(signal_ref, first_ref, second_ref, phase_ref, spectrum, turned):
        forward_body(signal_ref, first_ref, second_ref, phase_ref, spectrum, turned)

    vmem = pl.BlockSpec(memory_space=pltpu.VMEM)
    return pl.pallas_call(
        body,
        out_shape=pltpu.VMEM((SIDE, SIDE), jnp.float32),
        in_specs=[vmem] * 4,
        out_specs=vmem,
        scratch_shapes=[pltpu.VMEM((SIDE, 2 * SIDE), jnp.bfloat16)],
        compiler_params=pltpu.CompilerParams(vmem_limit_bytes=12 * MIB),
        name="forward",
    )(signal, first, second, factors)


def owners_of(segment, core, doubled):
    if not doubled:
        return [[0]]
    near, far = 2 - core, 1 + core
    masks = [[0, 4], [near, near ^ 4], [far, far ^ 4, far ^ near, far ^ near ^ 4]]
    return [[segment ^ mask for mask in block] for block in masks]


def inverse(spectrum, blocks, edges, third, fourth, phase, doubled):
    n_blocks = len(blocks)
    shard = blocks[0].shape[2]
    quarter = HALF // 2

    def body(*refs):
        spectrum_ref, block_refs = refs[0], refs[1 : 1 + n_blocks]
        edge_ref, third_ref, fourth_ref, phase_ref = refs[1 + n_blocks : 5 + n_blocks]
        snr_ref, chisq_ref, peak_ref = refs[5 + n_blocks : 8 + n_blocks]
        gathered, flipped, masked, turned, sums = refs[8 + n_blocks :]
        segment = lax.axis_index("segment")
        core = lax.axis_index("template")
        for block, owners in zip(block_refs, owners_of(segment, core, doubled), strict=True):
            for place, owner in enumerate(owners):
                here = pl.ds(pl.multiple_of(owner * shard, shard), shard)
                for part in range(2):
                    gathered[part, here, :] = block[place, part]
        for part in range(2):
            flipped[:, part * HALF : (part + 1) * HALF] = gathered[part].T
        edge = [edge_ref[:, number : number + 1] for number in range(3)]
        sums[...] = jnp.zeros_like(sums)
        step = 16

        def correlate(index):
            here = slice(index * step, (index + 1) * step)
            half, place = index // (HALF // step), index % (HALF // step)
            there = slice((2 * place + half) * step, (2 * place + half + 1) * step)
            spec_real = [spectrum_ref[here, q * quarter : (q + 1) * quarter] for q in range(2)]
            spec_imag = [spectrum_ref[here, (q + 2) * quarter : (q + 3) * quarter] for q in range(2)]
            temp_real = [
                flipped[here, q * quarter : (q + 1) * quarter].astype(jnp.float32) for q in range(2)
            ]
            temp_imag = [
                flipped[here, (q + 2) * quarter : (q + 3) * quarter].astype(jnp.float32)
                for q in range(2)
            ]
            lane = lax.broadcasted_iota(jnp.int32, (step, quarter), 1)
            base = lane * SIDE + lax.broadcasted_iota(jnp.int32, (step, quarter), 0) + index * step
            zero = jnp.zeros((step, quarter), jnp.float32)
            corr, above, power = [], [], []
            for q in range(2):
                corr.append(
                    (
                        spec_real[q] * temp_real[q] + spec_imag[q] * temp_imag[q],
                        spec_imag[q] * temp_real[q] - spec_real[q] * temp_imag[q],
                    )
                )
                power.append(temp_real[q] * temp_real[q] + temp_imag[q] * temp_imag[q])
                bins = base + q * quarter * SIDE
                above.append([bins >= edge[number] for number in range(3)])
            inside = [
                [~above[0][0], None],
                [above[0][0] & ~above[0][1], ~above[1][1]],
                [above[0][1] & ~above[0][2], above[1][1] & ~above[1][2]],
                [None, above[1][2]],
            ]
            inside[1][1] = ~above[1][1] & above[1][0]
            for number in range(4):
                first_half, second_half = inside[number]
                if second_half is None:
                    chosen = [jnp.where(first_half, corr[0][part], zero) for part in range(2)]
                    strength = jnp.where(first_half, power[0], zero)
                elif first_half is None:
                    chosen = [jnp.where(second_half, corr[1][part], zero) for part in range(2)]
                    strength = jnp.where(second_half, power[1], zero)
                else:
                    chosen = [
                        jnp.where(
                            first_half, corr[0][part], jnp.where(second_half, corr[1][part], zero)
                        )
                        for part in range(2)
                    ]
                    strength = jnp.where(first_half, power[0], zero) + jnp.where(
                        second_half, power[1], zero
                    )
                for part in range(2):
                    masked[number, there, part * quarter : (part + 1) * quarter] = chosen[
                        part
                    ].astype(jnp.bfloat16)
                folded = strength[0:8]
                for start in range(8, step, 8):
                    folded = folded + strength[start : start + 8]
                sums[number] += folded

        for index in range(SIDE // step):
            correlate(index)

        def first_pass(number, tile):
            product = jnp.dot(
                masked[number],
                third_ref[number, :, 2 * tile * 128 : 2 * (tile + 1) * 128],
                preferred_element_type=jnp.float32,
            ).reshape(HALF // step, 2, step, 2 * 128)
            lanes = slice(tile * 128, (tile + 1) * 128)
            real, imag = [], []
            for half in range(2):
                old_real, old_imag = (
                    product[:, half, :, part * 128 : (part + 1) * 128].astype(jnp.bfloat16)
                    for part in range(2)
                )
                cosine, sine = (
                    phase_ref[kind, half * HALF : (half + 1) * HALF, lanes].reshape(
                        HALF // step, step, 128
                    )
                    for kind in range(2)
                )
                real.append(old_real * cosine - old_imag * sine)
                imag.append(old_real * sine + old_imag * cosine)
            for part, (upper, lower) in enumerate((real, imag)):
                rows = slice(part * HALF, (part + 1) * HALF)
                columns = slice(number * 128, (number + 1) * 128)
                for parity, value in enumerate((upper + lower, upper - lower)):
                    turned[parity, tile, rows, columns] = value.reshape(HALF, 128)

        for number in range(4):
            for tile in range(SIDE // 128):
                first_pass(number, tile)

        bin_power = [jnp.sum(sums[number]) for number in range(4)]
        total = (bin_power[0] + bin_power[1]) + (bin_power[2] + bin_power[3])
        total_row = jnp.full((1, 128), total, jnp.float32)
        shares = [
            jnp.full((1, 128), bin_power[number], jnp.float32) / total_row for number in range(4)
        ]
        scale = (1.0 / LENGTH) / total_row

        def second_pass(tile, parity):
            product = jnp.dot(
                fourth_ref[parity], turned[parity, tile], preferred_element_type=jnp.float32
            ).reshape(quarter // 8, 2, 8, 4 * 128)
            real, imag = (
                [product[:, part, :, number * 128 : (number + 1) * 128] for number in range(4)]
                for part in range(2)
            )
            sum_real = (real[0] + real[1]) + (real[2] + real[3])
            sum_imag = (imag[0] + imag[1]) + (imag[2] + imag[3])
            snr = jnp.sqrt((sum_real * sum_real + sum_imag * sum_imag) * scale)
            chisq = None
            for number in range(4):
                diff_real = real[number] - shares[number] * sum_real
                diff_imag = imag[number] - shares[number] * sum_imag
                term = diff_real * diff_real + diff_imag * diff_imag
                chisq = term if chisq is None else chisq + term
            chisq = chisq * scale
            reduced = chisq * (1.0 / 6.0)
            inner = 0.5 + 0.5 * (reduced * reduced * reduced)
            weighted = snr * jnp.exp2(jnp.log2(inner) * (-1.0 / 6.0))
            newsnr = jnp.where(reduced > 1.0, weighted, snr)
            for kind, value in enumerate((snr, chisq)):
                rows = value.reshape(quarter, 128)
                for row in range(quarter):
                    place = (row * 2 * (SIDE // 128) + parity * (SIDE // 128) + tile) * 128
                    (snr_ref, chisq_ref)[kind][0, :, place : place + 128] = rows[
                        row : row + 1
                    ].astype(jnp.bfloat16)
            return jnp.max(newsnr.reshape(quarter, 128), axis=0, keepdims=True)

        peak = jnp.zeros((1, 128), jnp.float32)
        for tile in range(SIDE // 128):
            for parity in range(2):
                peak = jnp.maximum(peak, second_pass(tile, parity))
        peak_ref[...] = jnp.max(peak, axis=1, keepdims=True)

    vmem = pl.BlockSpec(memory_space=pltpu.VMEM)
    return pl.pallas_call(
        body,
        out_shape=(
            jax.ShapeDtypeStruct((1, 1, LENGTH // 2), jnp.bfloat16),
            jax.ShapeDtypeStruct((1, 1, LENGTH // 2), jnp.bfloat16),
            jax.ShapeDtypeStruct((1, 1), jnp.float32),
        ),
        in_specs=[vmem] * (5 + n_blocks),
        out_specs=(vmem, vmem, vmem),
        scratch_shapes=[
            pltpu.VMEM((2, HALF, SIDE), jnp.bfloat16),
            pltpu.VMEM((SIDE, SIDE), jnp.bfloat16),
            pltpu.VMEM((4, SIDE, HALF), jnp.bfloat16),
            pltpu.VMEM((2, SIDE // 128, SIDE, 4 * 128), jnp.bfloat16),
            pltpu.VMEM((4, 8, quarter), jnp.float32),
        ],
        compiler_params=pltpu.CompilerParams(vmem_limit_bytes=16 * MIB),
        name="inverse",
    )(spectrum, *blocks, *in_vmem(edges, third, fourth, phase))


def exchange(value, mesh_shape, mask_of):
    groups, segments, cores = (mesh_shape[name] for name in AXES)
    pairs = []
    for group in range(groups):
        for segment in range(segments):
            for core in range(cores):
                if mask_of(core):
                    here = (group * segments + segment) * cores + core
                    other = segment ^ mask_of(core)
                    pairs.append((here, (group * segments + other) * cores + core))
    return lax.ppermute(value, AXES, pairs)


def arrange_plain(strain_frames, frame_slot):
    count = lax.axis_size("segment")
    position = lax.axis_index("segment")
    frame_length = strain_frames.shape[1]
    counter = jnp.arange(count, dtype=jnp.int32)
    slot_now = lax.dynamic_slice_in_dim(frame_slot, position, 1, 1)[:, 0]
    next_index = jnp.minimum(position + 1, count - 1)
    slot_next = lax.dynamic_slice_in_dim(frame_slot, next_index, 1, 1)[:, 0]

    def arrange(slots, frames):
        selector = (counter[:, None] == slots[None, :]).astype(jnp.bfloat16)
        placed = jnp.dot(selector, frames, preferred_element_type=jnp.float32)
        return placed.astype(jnp.bfloat16).reshape(HALF, SIDE)

    following_rows = jnp.concatenate(
        [strain_frames[1:], jnp.zeros((1, frame_length), jnp.bfloat16)], axis=0
    )
    outgoing = jnp.stack([strain_frames, following_rows], axis=1)
    received = lax.all_to_all(outgoing, "segment", split_axis=0, concat_axis=0, tiled=True)
    leading = arrange(slot_now, received[:, 0])
    trailing = arrange(slot_next, received[:, 1])
    return jnp.concatenate([leading, trailing])


def local(mesh_shape, strain_frames, frame_slot, templates, bin_edges):
    constants = tables()
    count = mesh_shape["segment"]
    rows = strain_frames.shape[1] // SIDE
    staged = count == 8 and mesh_shape["template"] == 2 and rows % 16 == 0
    if staged:
        across = exchange(templates, mesh_shape, lambda core: 4)
        *outgoing, mine, unpacked = split_frames(strain_frames, templates)
        received = [
            exchange(value, mesh_shape, functools.partial(strain_mask, step))
            for step, value in enumerate(outgoing)
        ]
        pair = pair_shards(unpacked, across)
        near = exchange(pair, mesh_shape, lambda core: 2 - core)
        first, second, third, fourth, phase, factors = constants
        first, factors = load_tables((first, factors), pair)
        *received, first = lax.optimization_barrier((*received, first))
        other = lax.ppermute(jnp.stack(received), "template", [(0, 1), (1, 0)])
        far = exchange(jnp.concatenate([pair, near]), mesh_shape, lambda core: 1 + core)
        blocks = [pair, near, far]
        spectrum = forward_received(received, other, mine, frame_slot, first, second, factors)
    else:
        first, second, third, fourth, phase, factors = constants
        signal = arrange_plain(strain_frames, frame_slot)
        whole = lax.all_gather(templates, "segment", axis=2, tiled=True)
        blocks = [whole.reshape(1, 2, HALF, SIDE)]
        spectrum = forward_arranged(signal, first, second, factors)
    return inverse(spectrum, blocks, bin_edges, third, fourth, phase, staged)


def solution(mesh):
    mesh_shape = dict(mesh.shape)

    def step(strain_frames, frame_slot, templates, bin_edges):
        return local(mesh_shape, strain_frames, frame_slot, templates, bin_edges)

    in_specs = (
        P("segment", None),
        P(),
        P(("groups", "template"), None, "segment"),
        P(("groups", "template"), None),
    )
    out_specs = (
        P("segment", ("groups", "template"), None),
        P("segment", ("groups", "template"), None),
        P("segment", ("groups", "template")),
    )
    return jax.shard_map(step, mesh=mesh, in_specs=in_specs, out_specs=out_specs, check_vma=False)
```

```python
import functools
import math

import jax
import jax.numpy as jnp
import ml_dtypes
import numpy as np
from jax import lax
from jax.experimental import pallas as pl
from jax.experimental.pallas import tpu as pltpu
from jax.sharding import PartitionSpec as P

SIDE = 512
HALF = SIDE // 2
LENGTH = SIDE * SIDE
AXES = ("groups", "segment", "template")
MIB = 1 << 20
TINY = float(np.finfo(np.float32).tiny)
STEP = 16
BIN_LOW = (0, 32, 96, 128)
ROUNDS = 4
MASKS = ((7, 2, 1, 0), (3, 6, 5, 4))


def strain_mask(step, core):
    if isinstance(core, int):
        return MASKS[core][step]
    return jnp.where(core == 0, MASKS[0][step], MASKS[1][step])


def turn(rows, columns, modulus):
    product = np.outer(rows, columns) % modulus
    angles = 2.0 * math.pi / modulus * product.astype(np.float64)
    return np.cos(angles), np.sin(angles)


def tables():
    digit = np.arange(SIDE)
    cosine, sine = turn(digit, digit, SIDE)
    first = np.concatenate([cosine, -sine], axis=0)
    low = slice(0, HALF)
    second = np.block([[cosine[:, low], -sine[:, low]], [sine[:, low], cosine[:, low]]])
    third = []
    column = np.arange(HALF // 2)
    for start in BIN_LOW:
        chosen = np.where(column >= start, column, column + HALF // 2)
        real = np.concatenate([cosine[chosen], -sine[chosen]])
        imag = np.concatenate([sine[chosen], cosine[chosen]])
        tiles = np.stack([real, imag], axis=1).reshape(HALF, 2, SIDE // 128, 128)
        third.append(tiles.swapaxes(1, 2).reshape(HALF, 2 * SIDE))
    fourth = []
    for parity in range(2):
        kept = slice(HALF // 2 + parity, HALF // 2 + HALF, 2)
        real = np.concatenate([cosine[kept, low], -sine[kept, low]], axis=1)
        imag = np.concatenate([sine[kept, low], cosine[kept, low]], axis=1)
        pairs = np.stack([real.reshape(-1, 8, SIDE), imag.reshape(-1, 8, SIDE)], axis=1)
        fourth.append(pairs.reshape(HALF, SIDE))
    phase_cos, phase_sin = turn(digit, digit, LENGTH)
    phase = np.stack([phase_cos, phase_sin]).astype(np.float32).astype(ml_dtypes.bfloat16)
    coarse = [x[::STEP] for x in (phase_cos, phase_sin)]
    fine = [x[:STEP] for x in (phase_cos, phase_sin)]
    factors = np.concatenate([*coarse, *fine]).astype(np.float32)


    narrow = [x.astype(np.float32).astype(ml_dtypes.bfloat16) for x in (first, second, np.stack(third), np.stack(fourth))]
    return (*narrow, phase, factors)


def in_hbm(*arrays):
    return [pltpu.with_memory_space_constraint(x, pltpu.HBM) for x in arrays]


def in_vmem(*arrays):
    return [pltpu.with_memory_space_constraint(x, pltpu.VMEM) for x in arrays]


def spread(source, wide, count, rows):
    tiles = SIDE // 128
    for row in range(rows):
        for tile in range(tiles):
            place = (row * tiles + tile) * 128
            wide[tile, pl.ds(row, count, stride=rows), :] = source[:, place : place + 128].astype(
                jnp.float32
            )


def split_frames(frames, shard):
    count, samples = frames.shape
    rows = samples // SIDE
    tiles = SIDE // 128

    def body(frames_hbm, shard_hbm, *refs):
        outs, (unpacked, wide, narrow, frames_ref, shard_ref, arrived) = (
            refs[: ROUNDS + 1],
            refs[ROUNDS + 1 :],
        )
        copies = [
            pltpu.make_async_copy(frames_hbm, frames_ref, arrived.at[0]),
            pltpu.make_async_copy(shard_hbm, shard_ref, arrived.at[1]),
        ]
        for copy in copies:
            copy.start()
        segment = lax.axis_index("segment")
        core = lax.axis_index("template")
        wide[:, count * rows :, :] = jnp.zeros((tiles, rows, 128), jnp.float32)
        copies[0].wait()
        spread(frames_ref, wide, count, rows)
        for step, out_ref in enumerate(outs):
            mask = strain_mask(step, core) if step < ROUNDS else 0
            start = pl.multiple_of((segment ^ mask) * rows, rows)
            for tile in range(tiles):
                out_ref[:, :, tile * 128 : tile * 128 + 128] = (
                    wide[tile, pl.ds(start, 2 * rows), :].astype(jnp.bfloat16).reshape(2, rows, 128)
                )
        copies[1].wait()
        unpack(shard_ref, narrow, unpacked.at[0])

    vmem = pl.BlockSpec(memory_space=pltpu.VMEM)
    return pl.pallas_call(
        body,
        out_shape=[pltpu.VMEM((2, rows, SIDE), jnp.bfloat16)] * (ROUNDS + 1)
        + [pltpu.VMEM((1, 2, rows, SIDE), jnp.bfloat16)],
        in_specs=[pl.BlockSpec(memory_space=pl.ANY)] * 2,
        out_specs=[vmem] * (ROUNDS + 2),
        scratch_shapes=[
            pltpu.VMEM((tiles, (count + 1) * rows, 128), jnp.float32),
            pltpu.VMEM((tiles, 2 * rows, 128), jnp.float32),
            pltpu.VMEM(frames.shape, frames.dtype),
            pltpu.VMEM(shard.shape, shard.dtype),
            pltpu.SemaphoreType.DMA((2,)),
        ],
        compiler_params=pltpu.CompilerParams(vmem_limit_bytes=4 * MIB),
        name="split_frames",
    )(*in_hbm(frames, shard))


def unpack(shard_ref, narrow, out_ref):
    rows = out_ref.shape[1]
    spread(shard_ref.at[0], narrow, 2, rows)
    for tile in range(SIDE // 128):
        out_ref[:, :, tile * 128 : tile * 128 + 128] = (
            narrow[tile].astype(jnp.bfloat16).reshape(2, rows, 128)
        )


def pair_shards(unpacked, across):
    rows = unpacked.shape[2]

    def body(unpacked_ref, across_ref, out_ref, narrow):
        out_ref[0] = unpacked_ref[0]
        unpack(across_ref, narrow, out_ref.at[1])

    vmem = pl.BlockSpec(memory_space=pltpu.VMEM)
    return pl.pallas_call(
        body,
        out_shape=pltpu.VMEM((2, 2, rows, SIDE), jnp.bfloat16),
        in_specs=[vmem, vmem],
        out_specs=vmem,
        scratch_shapes=[pltpu.VMEM((SIDE // 128, 2 * rows, 128), jnp.float32)],
        compiler_params=pltpu.CompilerParams(vmem_limit_bytes=4 * MIB),
        name="pair_shards",
    )(unpacked, across)


def load_tables(arrays, after):
    count = len(arrays)

    def body(*refs):
        sources, outs, arrived = refs[:count], refs[count + 1 : 2 * count + 1], refs[-1]
        copies = [
            pltpu.make_async_copy(source, out, arrived.at[place])
            for place, (source, out) in enumerate(zip(sources, outs, strict=True))
        ]
        for copy in copies:
            copy.start()
        for copy in copies:
            copy.wait()

    hbm = pl.BlockSpec(memory_space=pl.ANY)
    return pl.pallas_call(
        body,
        out_shape=[pltpu.VMEM(x.shape, x.dtype) for x in arrays],
        in_specs=[hbm] * (count + 1),
        out_specs=[pl.BlockSpec(memory_space=pltpu.VMEM)] * count,
        scratch_shapes=[pltpu.SemaphoreType.DMA((count,))],
        compiler_params=pltpu.CompilerParams(vmem_limit_bytes=1 * MIB),
        name="load_tables",
    )(*in_hbm(*arrays), after)


def phases(factors, first, count):
    groups = SIDE // STEP
    coarse_cos, coarse_sin = (
        factors[pl.ds(kind * groups + first, count), :][:, None, :] for kind in range(2)
    )
    fine_cos, fine_sin = (
        factors[2 * groups + kind * STEP : 2 * groups + (kind + 1) * STEP, :][None]
        for kind in range(2)
    )
    cosine = coarse_cos * fine_cos - coarse_sin * fine_sin
    sine = coarse_sin * fine_cos + coarse_cos * fine_sin
    return cosine.reshape(count * STEP, SIDE), sine.reshape(count * STEP, SIDE)


def forward_body(signal, first, second, factors, spectrum, turned):
    rows = SIDE // 2

    def chunk(index):
        here = pl.ds(index * rows, rows)
        there = pl.ds(SIDE + index * rows, rows)
        real = jnp.dot(first[here, :], signal[...], preferred_element_type=jnp.float32)
        imag = jnp.dot(first[there, :], signal[...], preferred_element_type=jnp.float32)
        cosine, sine = phases(factors, index * (rows // STEP), rows // STEP)
        turned[here, :SIDE] = (real * cosine + imag * sine).astype(jnp.bfloat16)
        turned[here, SIDE:] = (imag * cosine - real * sine).astype(jnp.bfloat16)
        spectrum[here, :] = jnp.dot(
            turned[here, :], second[...], preferred_element_type=jnp.float32
        )

    for index in range(SIDE // rows):
        chunk(index)


def forward_received(received, other, mine, frame_slot, first, second, factors):
    rows = mine.shape[1]

    def body(*refs):
        received_refs, other_ref, mine_ref, slot_ref = refs[:ROUNDS], *refs[ROUNDS : ROUNDS + 3]
        first_ref, second_ref, phase_ref, spectrum, signal, turned = refs[ROUNDS + 3 :]
        segment = lax.axis_index("segment")
        core = lax.axis_index("template")
        following = jnp.minimum(segment + 1, slot_ref.shape[1] - 1)

        def place(source, frames):
            for part, half in enumerate((segment, following)):
                start = part * HALF + slot_ref[source, half] * rows
                signal[pl.ds(pl.multiple_of(start, rows), rows), :] = frames[part]

        for step in range(ROUNDS):
            place(segment ^ strain_mask(step, core), received_refs[step])
            place(segment ^ strain_mask(step, 1 - core), other_ref.at[step])
        place(segment, mine_ref)
        forward_body(signal, first_ref, second_ref, phase_ref, spectrum, turned)

    vmem = pl.BlockSpec(memory_space=pltpu.VMEM)
    return pl.pallas_call(
        body,
        out_shape=pltpu.VMEM((SIDE, SIDE), jnp.float32),
        in_specs=[vmem] * (ROUNDS + 2) + [pl.BlockSpec(memory_space=pltpu.SMEM)] + [vmem] * 3,
        out_specs=vmem,
        scratch_shapes=[
            pltpu.VMEM((SIDE, SIDE), jnp.bfloat16),
            pltpu.VMEM((SIDE, 2 * SIDE), jnp.bfloat16),
        ],
        compiler_params=pltpu.CompilerParams(vmem_limit_bytes=12 * MIB),
        cost_estimate=pl.CostEstimate(
            flops=4 * SIDE**3 * 2, bytes_accessed=6 * MIB, transcendentals=0
        ),
        name="forward",
    )(*received, other, mine, frame_slot, first, *in_vmem(second), factors)


def forward_arranged(signal, first, second, factors):
    def body(signal_ref, first_ref, second_ref, phase_ref, spectrum, turned):
        forward_body(signal_ref, first_ref, second_ref, phase_ref, spectrum, turned)

    vmem = pl.BlockSpec(memory_space=pltpu.VMEM)
    return pl.pallas_call(
        body,
        out_shape=pltpu.VMEM((SIDE, SIDE), jnp.float32),
        in_specs=[vmem] * 4,
        out_specs=vmem,
        scratch_shapes=[pltpu.VMEM((SIDE, 2 * SIDE), jnp.bfloat16)],
        compiler_params=pltpu.CompilerParams(vmem_limit_bytes=12 * MIB),
        name="forward",
    )(signal, first, second, factors)


def owners_of(segment, core, doubled):
    if not doubled:
        return [[0]]
    near, far = 1 + core, 2 - core
    masks = [[0, 4], [near, near ^ 4], [far, far ^ 4, far ^ near, far ^ near ^ 4]]
    return [[segment ^ mask for mask in block] for block in masks]


def inverse(spectrum, blocks, edges, third, fourth, phase, doubled):
    n_blocks = len(blocks)
    shard = blocks[0].shape[2]
    quarter = HALF // 2

    def body(*refs):
        spectrum_ref, block_refs = refs[0], refs[1 : 1 + n_blocks]
        edge_ref, third_ref, fourth_ref, phase_ref = refs[1 + n_blocks : 5 + n_blocks]
        snr_ref, chisq_ref, peak_ref = refs[5 + n_blocks : 8 + n_blocks]
        gathered, flipped, masked, turned, sums = refs[8 + n_blocks :]
        segment = lax.axis_index("segment")
        core = lax.axis_index("template")
        for block, owners in zip(block_refs, owners_of(segment, core, doubled), strict=True):
            for place, owner in enumerate(owners):
                here = pl.ds(pl.multiple_of(owner * shard, shard), shard)
                for part in range(2):
                    gathered[part, here, :] = block[place, part]
        for part in range(2):
            flipped[:, part * HALF : (part + 1) * HALF] = gathered[part].T
        edge = [edge_ref[:, number : number + 1] for number in range(3)]
        sums[...] = jnp.zeros_like(sums)
        step = 16

        def correlate(index):
            here = slice(index * step, (index + 1) * step)
            half, place = index // (HALF // step), index % (HALF // step)
            there = slice((2 * place + half) * step, (2 * place + half + 1) * step)
            spec_real = [spectrum_ref[here, q * quarter : (q + 1) * quarter] for q in range(2)]
            spec_imag = [spectrum_ref[here, (q + 2) * quarter : (q + 3) * quarter] for q in range(2)]
            temp_real = [
                flipped[here, q * quarter : (q + 1) * quarter].astype(jnp.float32) for q in range(2)
            ]
            temp_imag = [
                flipped[here, (q + 2) * quarter : (q + 3) * quarter].astype(jnp.float32)
                for q in range(2)
            ]
            lane = lax.broadcasted_iota(jnp.int32, (step, quarter), 1)
            base = lane * SIDE + lax.broadcasted_iota(jnp.int32, (step, quarter), 0) + index * step
            zero = jnp.zeros((step, quarter), jnp.float32)
            corr, above, power = [], [], []
            for q in range(2):
                corr.append(
                    (
                        spec_real[q] * temp_real[q] + spec_imag[q] * temp_imag[q],
                        spec_imag[q] * temp_real[q] - spec_real[q] * temp_imag[q],
                    )
                )
                power.append(temp_real[q] * temp_real[q] + temp_imag[q] * temp_imag[q])
                bins = base + q * quarter * SIDE
                above.append([bins >= edge[number] for number in range(3)])
            inside = [
                [~above[0][0], None],
                [above[0][0] & ~above[0][1], ~above[1][1]],
                [above[0][1] & ~above[0][2], above[1][1] & ~above[1][2]],
                [None, above[1][2]],
            ]
            inside[1][1] = ~above[1][1] & above[1][0]
            for number in range(4):
                first_half, second_half = inside[number]
                if second_half is None:
                    chosen = [jnp.where(first_half, corr[0][part], zero) for part in range(2)]
                    strength = jnp.where(first_half, power[0], zero)
                elif first_half is None:
                    chosen = [jnp.where(second_half, corr[1][part], zero) for part in range(2)]
                    strength = jnp.where(second_half, power[1], zero)
                else:
                    chosen = [
                        jnp.where(
                            first_half, corr[0][part], jnp.where(second_half, corr[1][part], zero)
                        )
                        for part in range(2)
                    ]
                    strength = jnp.where(first_half, power[0], zero) + jnp.where(
                        second_half, power[1], zero
                    )
                for part in range(2):
                    masked[number, there, part * quarter : (part + 1) * quarter] = chosen[
                        part
                    ].astype(jnp.bfloat16)
                folded = strength[0:8]
                for start in range(8, step, 8):
                    folded = folded + strength[start : start + 8]
                sums[number] += folded

        for index in range(SIDE // step):
            correlate(index)

        def first_pass(number, tile):
            product = jnp.dot(
                masked[number],
                third_ref[number, :, 2 * tile * 128 : 2 * (tile + 1) * 128],
                preferred_element_type=jnp.float32,
            ).reshape(HALF // step, 2, step, 2 * 128)
            lanes = slice(tile * 128, (tile + 1) * 128)
            real, imag = [], []
            for half in range(2):
                old_real, old_imag = (
                    product[:, half, :, part * 128 : (part + 1) * 128].astype(jnp.bfloat16)
                    for part in range(2)
                )
                cosine, sine = (
                    phase_ref[kind, half * HALF : (half + 1) * HALF, lanes].reshape(
                        HALF // step, step, 128
                    )
                    for kind in range(2)
                )
                real.append(old_real * cosine - old_imag * sine)
                imag.append(old_real * sine + old_imag * cosine)
            for part, (upper, lower) in enumerate((real, imag)):
                rows = slice(part * HALF, (part + 1) * HALF)
                columns = slice(number * 128, (number + 1) * 128)
                for parity, value in enumerate((upper + lower, upper - lower)):
                    turned[parity, tile, rows, columns] = value.reshape(HALF, 128)

        for number in range(4):
            for tile in range(SIDE // 128):
                first_pass(number, tile)

        bin_power = [jnp.sum(sums[number]) for number in range(4)]
        total = (bin_power[0] + bin_power[1]) + (bin_power[2] + bin_power[3])
        total_row = jnp.full((1, 128), total, jnp.float32)
        shares = [
            jnp.full((1, 128), bin_power[number], jnp.float32) / total_row for number in range(4)
        ]
        scale = (1.0 / LENGTH) / total_row

        def second_pass(tile, parity):
            product = jnp.dot(
                fourth_ref[parity], turned[parity, tile], preferred_element_type=jnp.float32
            ).reshape(quarter // 8, 2, 8, 4 * 128)
            real, imag = (
                [product[:, part, :, number * 128 : (number + 1) * 128] for number in range(4)]
                for part in range(2)
            )
            sum_real = (real[0] + real[1]) + (real[2] + real[3])
            sum_imag = (imag[0] + imag[1]) + (imag[2] + imag[3])
            square = (sum_real * sum_real + sum_imag * sum_imag) * scale
            snr = square * lax.rsqrt(jnp.maximum(square, TINY))
            chisq = None
            for number in range(4):
                diff_real = real[number] - shares[number] * sum_real
                diff_imag = imag[number] - shares[number] * sum_imag
                term = diff_real * diff_real + diff_imag * diff_imag
                chisq = term if chisq is None else chisq + term
            chisq = chisq * scale
            reduced = chisq * (1.0 / 6.0)
            reduced = jnp.maximum(reduced, 1.0)
            inner = 0.5 + 0.5 * (reduced * reduced * reduced)
            newsnr = snr * jnp.exp2(jnp.log2(inner) * (-1.0 / 6.0))
            for kind, value in enumerate((snr, chisq)):
                rows = value.reshape(quarter, 128)
                for row in range(quarter):
                    place = (row * 2 * (SIDE // 128) + parity * (SIDE // 128) + tile) * 128
                    (snr_ref, chisq_ref)[kind][0, :, place : place + 128] = rows[
                        row : row + 1
                    ].astype(jnp.bfloat16)
            return jnp.max(newsnr.reshape(quarter, 128), axis=0, keepdims=True)

        peak = jnp.zeros((1, 128), jnp.float32)
        for tile in range(SIDE // 128):
            for parity in range(2):
                peak = jnp.maximum(peak, second_pass(tile, parity))
        peak_ref[...] = jnp.max(peak, axis=1, keepdims=True)

    vmem = pl.BlockSpec(memory_space=pltpu.VMEM)
    return pl.pallas_call(
        body,
        out_shape=(
            jax.ShapeDtypeStruct((1, 1, LENGTH // 2), jnp.bfloat16),
            jax.ShapeDtypeStruct((1, 1, LENGTH // 2), jnp.bfloat16),
            jax.ShapeDtypeStruct((1, 1), jnp.float32),
        ),
        in_specs=[vmem] * (5 + n_blocks),
        out_specs=(vmem, vmem, vmem),
        scratch_shapes=[
            pltpu.VMEM((2, HALF, SIDE), jnp.bfloat16),
            pltpu.VMEM((SIDE, SIDE), jnp.bfloat16),
            pltpu.VMEM((4, SIDE, HALF), jnp.bfloat16),
            pltpu.VMEM((2, SIDE // 128, SIDE, 4 * 128), jnp.bfloat16),
            pltpu.VMEM((4, 8, quarter), jnp.float32),
        ],
        compiler_params=pltpu.CompilerParams(vmem_limit_bytes=16 * MIB),
        name="inverse",
    )(spectrum, *blocks, *in_vmem(edges, third, fourth, phase))


def exchange(value, mesh_shape, mask_of):
    groups, segments, cores = (mesh_shape[name] for name in AXES)
    pairs = []
    for group in range(groups):
        for segment in range(segments):
            for core in range(cores):
                if mask_of(core):
                    here = (group * segments + segment) * cores + core
                    other = segment ^ mask_of(core)
                    pairs.append((here, (group * segments + other) * cores + core))
    return lax.ppermute(value, AXES, pairs)


def arrange_plain(strain_frames, frame_slot):
    count = lax.axis_size("segment")
    position = lax.axis_index("segment")
    frame_length = strain_frames.shape[1]
    counter = jnp.arange(count, dtype=jnp.int32)
    slot_now = lax.dynamic_slice_in_dim(frame_slot, position, 1, 1)[:, 0]
    next_index = jnp.minimum(position + 1, count - 1)
    slot_next = lax.dynamic_slice_in_dim(frame_slot, next_index, 1, 1)[:, 0]

    def arrange(slots, frames):
        selector = (counter[:, None] == slots[None, :]).astype(jnp.bfloat16)
        placed = jnp.dot(selector, frames, preferred_element_type=jnp.float32)
        return placed.astype(jnp.bfloat16).reshape(HALF, SIDE)

    following_rows = jnp.concatenate(
        [strain_frames[1:], jnp.zeros((1, frame_length), jnp.bfloat16)], axis=0
    )
    outgoing = jnp.stack([strain_frames, following_rows], axis=1)
    received = lax.all_to_all(outgoing, "segment", split_axis=0, concat_axis=0, tiled=True)
    leading = arrange(slot_now, received[:, 0])
    trailing = arrange(slot_next, received[:, 1])
    return jnp.concatenate([leading, trailing])


def local(mesh_shape, strain_frames, frame_slot, templates, bin_edges):
    constants = tables()
    count = mesh_shape["segment"]
    rows = strain_frames.shape[1] // SIDE
    staged = count == 8 and mesh_shape["template"] == 2 and rows % 16 == 0
    if staged:
        across = exchange(templates, mesh_shape, lambda core: 4)
        *outgoing, mine, unpacked = split_frames(strain_frames, templates)
        received = [
            exchange(value, mesh_shape, functools.partial(strain_mask, step))
            for step, value in enumerate(outgoing)
        ]
        pair = pair_shards(unpacked, across)
        near = exchange(pair, mesh_shape, lambda core: 1 + core)
        first, second, third, fourth, phase, factors = constants
        first, factors = load_tables((first, factors), pair)
        *received, first = lax.optimization_barrier((*received, first))
        other = lax.ppermute(jnp.stack(received), "template", [(0, 1), (1, 0)])
        far = exchange(jnp.concatenate([pair, near]), mesh_shape, lambda core: 2 - core)
        blocks = [pair, near, far]
        spectrum = forward_received(received, other, mine, frame_slot, first, second, factors)
    else:
        first, second, third, fourth, phase, factors = constants
        signal = arrange_plain(strain_frames, frame_slot)
        whole = lax.all_gather(templates, "segment", axis=2, tiled=True)
        blocks = [whole.reshape(1, 2, HALF, SIDE)]
        spectrum = forward_arranged(signal, first, second, factors)
    return inverse(spectrum, blocks, bin_edges, third, fourth, phase, staged)


def solution(mesh):
    mesh_shape = dict(mesh.shape)

    def step(strain_frames, frame_slot, templates, bin_edges):
        return local(mesh_shape, strain_frames, frame_slot, templates, bin_edges)

    in_specs = (
        P("segment", None),
        P(),
        P(("groups", "template"), None, "segment"),
        P(("groups", "template"), None),
    )
    out_specs = (
        P("segment", ("groups", "template"), None),
        P("segment", ("groups", "template"), None),
        P("segment", ("groups", "template")),
    )
    return jax.shard_map(step, mesh=mesh, in_specs=in_specs, out_specs=out_specs, check_vma=False)
```

```python
import functools
import math

import jax
import jax.numpy as jnp
import ml_dtypes
import numpy as np
from jax import lax
from jax.experimental import pallas as pl
from jax.experimental.pallas import tpu as pltpu
from jax.sharding import PartitionSpec as P

SIDE = 512
HALF = SIDE // 2
LENGTH = SIDE * SIDE
AXES = ("groups", "segment", "template")
MIB = 1 << 20
TINY = float(np.finfo(np.float32).tiny)
STEP = 16
BIN_LOW = (0, 32, 96, 128)
ROUNDS = 4
MASKS = ((7, 2, 1, 0), (3, 6, 5, 4))


def strain_mask(step, core):
    if isinstance(core, int):
        return MASKS[core][step]
    return jnp.where(core == 0, MASKS[0][step], MASKS[1][step])


def turn(rows, columns, modulus):
    product = np.outer(rows, columns) % modulus
    angles = 2.0 * math.pi / modulus * product.astype(np.float64)
    return np.cos(angles), np.sin(angles)


def tables():
    digit = np.arange(SIDE)
    cosine, sine = turn(digit, digit, SIDE)
    first = np.concatenate([cosine, -sine], axis=0)
    low = slice(0, HALF)
    second = np.block([[cosine[:, low], -sine[:, low]], [sine[:, low], cosine[:, low]]])
    third = []
    column = np.arange(HALF // 2)
    for start in BIN_LOW:
        chosen = np.where(column >= start, column, column + HALF // 2)
        real = np.concatenate([cosine[chosen], -sine[chosen]])
        imag = np.concatenate([sine[chosen], cosine[chosen]])
        tiles = np.stack([real, imag], axis=1).reshape(HALF, 2, SIDE // 128, 128)
        third.append(tiles.swapaxes(1, 2).reshape(HALF, 2 * SIDE))
    fourth = []
    for parity in range(2):
        kept = slice(HALF // 2 + parity, HALF // 2 + HALF, 2)
        real = np.concatenate([cosine[kept, low], -sine[kept, low]], axis=1)
        imag = np.concatenate([sine[kept, low], cosine[kept, low]], axis=1)
        pairs = np.stack([real.reshape(-1, 8, SIDE), imag.reshape(-1, 8, SIDE)], axis=1)
        fourth.append(pairs.reshape(HALF, SIDE))
    phase_cos, phase_sin = turn(digit, digit, LENGTH)
    phase = np.stack([phase_cos, phase_sin]).astype(np.float32).astype(ml_dtypes.bfloat16)
    coarse = [x[::STEP] for x in (phase_cos, phase_sin)]
    fine = [x[:STEP] for x in (phase_cos, phase_sin)]
    factors = np.concatenate([*coarse, *fine]).astype(np.float32)


    narrow = [x.astype(np.float32).astype(ml_dtypes.bfloat16) for x in (first, second, np.stack(third), np.stack(fourth))]
    return (*narrow, phase, factors)


def in_hbm(*arrays):
    return [pltpu.with_memory_space_constraint(x, pltpu.HBM) for x in arrays]


def in_vmem(*arrays):
    return [pltpu.with_memory_space_constraint(x, pltpu.VMEM) for x in arrays]


def spread(source, wide, count, rows):
    tiles = SIDE // 128
    for row in range(rows):
        for tile in range(tiles):
            place = (row * tiles + tile) * 128
            wide[tile, pl.ds(row, count, stride=rows), :] = source[:, place : place + 128].astype(
                jnp.float32
            )


def split_frames(frames, shard):
    count, samples = frames.shape
    rows = samples // SIDE
    tiles = SIDE // 128

    def body(frames_hbm, shard_hbm, *refs):
        outs, (unpacked, wide, narrow, frames_ref, shard_ref, arrived) = (
            refs[: ROUNDS + 1],
            refs[ROUNDS + 1 :],
        )
        copies = [
            pltpu.make_async_copy(frames_hbm, frames_ref, arrived.at[0]),
            pltpu.make_async_copy(shard_hbm, shard_ref, arrived.at[1]),
        ]
        for copy in copies:
            copy.start()
        segment = lax.axis_index("segment")
        core = lax.axis_index("template")
        wide[:, count * rows :, :] = jnp.zeros((tiles, rows, 128), jnp.float32)
        copies[0].wait()
        spread(frames_ref, wide, count, rows)
        for step, out_ref in enumerate(outs):
            mask = strain_mask(step, core) if step < ROUNDS else 0
            start = pl.multiple_of((segment ^ mask) * rows, rows)
            for tile in range(tiles):
                out_ref[:, :, tile * 128 : tile * 128 + 128] = (
                    wide[tile, pl.ds(start, 2 * rows), :].astype(jnp.bfloat16).reshape(2, rows, 128)
                )
        copies[1].wait()
        unpack(shard_ref, narrow, unpacked.at[0])

    vmem = pl.BlockSpec(memory_space=pltpu.VMEM)
    return pl.pallas_call(
        body,
        out_shape=[pltpu.VMEM((2, rows, SIDE), jnp.bfloat16)] * (ROUNDS + 1)
        + [pltpu.VMEM((1, 2, rows, SIDE), jnp.bfloat16)],
        in_specs=[pl.BlockSpec(memory_space=pl.ANY)] * 2,
        out_specs=[vmem] * (ROUNDS + 2),
        scratch_shapes=[
            pltpu.VMEM((tiles, (count + 1) * rows, 128), jnp.float32),
            pltpu.VMEM((tiles, 2 * rows, 128), jnp.float32),
            pltpu.VMEM(frames.shape, frames.dtype),
            pltpu.VMEM(shard.shape, shard.dtype),
            pltpu.SemaphoreType.DMA((2,)),
        ],
        compiler_params=pltpu.CompilerParams(vmem_limit_bytes=4 * MIB),
        name="split_frames",
    )(*in_hbm(frames, shard))


def unpack(shard_ref, narrow, out_ref):
    rows = out_ref.shape[1]
    spread(shard_ref.at[0], narrow, 2, rows)
    for tile in range(SIDE // 128):
        out_ref[:, :, tile * 128 : tile * 128 + 128] = (
            narrow[tile].astype(jnp.bfloat16).reshape(2, rows, 128)
        )


def pair_shards(unpacked, across):
    rows = unpacked.shape[2]

    def body(unpacked_ref, across_ref, out_ref, narrow):
        out_ref[0] = unpacked_ref[0]
        unpack(across_ref, narrow, out_ref.at[1])

    vmem = pl.BlockSpec(memory_space=pltpu.VMEM)
    return pl.pallas_call(
        body,
        out_shape=pltpu.VMEM((2, 2, rows, SIDE), jnp.bfloat16),
        in_specs=[vmem, vmem],
        out_specs=vmem,
        scratch_shapes=[pltpu.VMEM((SIDE // 128, 2 * rows, 128), jnp.float32)],
        compiler_params=pltpu.CompilerParams(vmem_limit_bytes=4 * MIB),
        name="pair_shards",
    )(unpacked, across)


def load_tables(arrays, after):
    count = len(arrays)

    def body(*refs):
        sources, outs, arrived = refs[:count], refs[count + 1 : 2 * count + 1], refs[-1]
        copies = [
            pltpu.make_async_copy(source, out, arrived.at[place])
            for place, (source, out) in enumerate(zip(sources, outs, strict=True))
        ]
        for copy in copies:
            copy.start()
        for copy in copies:
            copy.wait()

    hbm = pl.BlockSpec(memory_space=pl.ANY)
    return pl.pallas_call(
        body,
        out_shape=[pltpu.VMEM(x.shape, x.dtype) for x in arrays],
        in_specs=[hbm] * (count + 1),
        out_specs=[pl.BlockSpec(memory_space=pltpu.VMEM)] * count,
        scratch_shapes=[pltpu.SemaphoreType.DMA((count,))],
        compiler_params=pltpu.CompilerParams(vmem_limit_bytes=1 * MIB),
        name="load_tables",
    )(*in_hbm(*arrays), after)


def phases(factors, first, count):
    groups = SIDE // STEP
    coarse_cos, coarse_sin = (
        factors[pl.ds(kind * groups + first, count), :][:, None, :] for kind in range(2)
    )
    fine_cos, fine_sin = (
        factors[2 * groups + kind * STEP : 2 * groups + (kind + 1) * STEP, :][None]
        for kind in range(2)
    )
    cosine = coarse_cos * fine_cos - coarse_sin * fine_sin
    sine = coarse_sin * fine_cos + coarse_cos * fine_sin
    return cosine.reshape(count * STEP, SIDE), sine.reshape(count * STEP, SIDE)


def forward_body(signal, first, second, factors, spectrum, turned):
    rows = SIDE // 2

    def chunk(index):
        here = pl.ds(index * rows, rows)
        there = pl.ds(SIDE + index * rows, rows)
        real = jnp.dot(first[here, :], signal[...], preferred_element_type=jnp.float32)
        imag = jnp.dot(first[there, :], signal[...], preferred_element_type=jnp.float32)
        cosine, sine = phases(factors, index * (rows // STEP), rows // STEP)
        turned[here, :SIDE] = (real * cosine + imag * sine).astype(jnp.bfloat16)
        turned[here, SIDE:] = (imag * cosine - real * sine).astype(jnp.bfloat16)
        spectrum[here, :] = jnp.dot(
            turned[here, :], second[...], preferred_element_type=jnp.float32
        )

    for index in range(SIDE // rows):
        chunk(index)


def forward_received(received, other, mine, frame_slot, first, second, factors):
    rows = mine.shape[1]

    def body(*refs):
        received_refs, other_ref, mine_ref, slot_ref = refs[:ROUNDS], *refs[ROUNDS : ROUNDS + 3]
        first_ref, second_ref, phase_ref, spectrum, signal, turned = refs[ROUNDS + 3 :]
        segment = lax.axis_index("segment")
        core = lax.axis_index("template")
        following = jnp.minimum(segment + 1, slot_ref.shape[1] - 1)

        def place(source, frames):
            for part, half in enumerate((segment, following)):
                start = part * HALF + slot_ref[source, half] * rows
                signal[pl.ds(pl.multiple_of(start, rows), rows), :] = frames[part]

        for step in range(ROUNDS):
            place(segment ^ strain_mask(step, core), received_refs[step])
            place(segment ^ strain_mask(step, 1 - core), other_ref.at[step])
        place(segment, mine_ref)
        forward_body(signal, first_ref, second_ref, phase_ref, spectrum, turned)

    vmem = pl.BlockSpec(memory_space=pltpu.VMEM)
    return pl.pallas_call(
        body,
        out_shape=pltpu.VMEM((SIDE, SIDE), jnp.float32),
        in_specs=[vmem] * (ROUNDS + 2) + [pl.BlockSpec(memory_space=pltpu.SMEM)] + [vmem] * 3,
        out_specs=vmem,
        scratch_shapes=[
            pltpu.VMEM((SIDE, SIDE), jnp.bfloat16),
            pltpu.VMEM((SIDE, 2 * SIDE), jnp.bfloat16),
        ],
        compiler_params=pltpu.CompilerParams(vmem_limit_bytes=12 * MIB),
        cost_estimate=pl.CostEstimate(
            flops=4 * SIDE**3 * 2, bytes_accessed=6 * MIB, transcendentals=0
        ),
        name="forward",
    )(*received, other, mine, frame_slot, first, *in_vmem(second), factors)


def forward_arranged(signal, first, second, factors):
    def body(signal_ref, first_ref, second_ref, phase_ref, spectrum, turned):
        forward_body(signal_ref, first_ref, second_ref, phase_ref, spectrum, turned)

    vmem = pl.BlockSpec(memory_space=pltpu.VMEM)
    return pl.pallas_call(
        body,
        out_shape=pltpu.VMEM((SIDE, SIDE), jnp.float32),
        in_specs=[vmem] * 4,
        out_specs=vmem,
        scratch_shapes=[pltpu.VMEM((SIDE, 2 * SIDE), jnp.bfloat16)],
        compiler_params=pltpu.CompilerParams(vmem_limit_bytes=12 * MIB),
        name="forward",
    )(signal, first, second, factors)


def owners_of(segment, core, doubled):
    if not doubled:
        return [[0]]
    near, far = 1 + core, 2 - core
    masks = [[0, 4], [near, near ^ 4], [far, far ^ 4, far ^ near, far ^ near ^ 4]]
    return [[segment ^ mask for mask in block] for block in masks]


def inverse(spectrum, blocks, edges, third, fourth, phase, doubled):
    n_blocks = len(blocks)
    shard = blocks[0].shape[2]
    quarter = HALF // 2

    def body(*refs):
        spectrum_ref, block_refs = refs[0], refs[1 : 1 + n_blocks]
        edge_ref, third_ref, fourth_ref, phase_ref = refs[1 + n_blocks : 5 + n_blocks]
        snr_ref, chisq_ref, peak_ref = refs[5 + n_blocks : 8 + n_blocks]
        gathered, flipped, masked, turned, sums = refs[8 + n_blocks :]
        segment = lax.axis_index("segment")
        core = lax.axis_index("template")
        for block, owners in zip(block_refs, owners_of(segment, core, doubled), strict=True):
            for place, owner in enumerate(owners):
                here = pl.ds(pl.multiple_of(owner * shard, shard), shard)
                for part in range(2):
                    gathered[part, here, :] = block[place, part]
        for part in range(2):
            flipped[:, part * HALF : (part + 1) * HALF] = gathered[part].T
        edge = [edge_ref[:, number : number + 1] for number in range(3)]
        sums[...] = jnp.zeros_like(sums)
        step = 16

        def correlate(index):
            here = slice(index * step, (index + 1) * step)
            half, place = index // (HALF // step), index % (HALF // step)
            there = slice((2 * place + half) * step, (2 * place + half + 1) * step)
            spec_real = [spectrum_ref[here, q * quarter : (q + 1) * quarter] for q in range(2)]
            spec_imag = [spectrum_ref[here, (q + 2) * quarter : (q + 3) * quarter] for q in range(2)]
            temp_real = [
                flipped[here, q * quarter : (q + 1) * quarter].astype(jnp.float32) for q in range(2)
            ]
            temp_imag = [
                flipped[here, (q + 2) * quarter : (q + 3) * quarter].astype(jnp.float32)
                for q in range(2)
            ]
            lane = lax.broadcasted_iota(jnp.int32, (step, quarter), 1)
            base = lane * SIDE + lax.broadcasted_iota(jnp.int32, (step, quarter), 0) + index * step
            zero = jnp.zeros((step, quarter), jnp.float32)
            corr, above, power = [], [], []
            for q in range(2):
                corr.append(
                    (
                        spec_real[q] * temp_real[q] + spec_imag[q] * temp_imag[q],
                        spec_imag[q] * temp_real[q] - spec_real[q] * temp_imag[q],
                    )
                )
                power.append(temp_real[q] * temp_real[q] + temp_imag[q] * temp_imag[q])
                bins = base + q * quarter * SIDE
                above.append([bins >= edge[number] for number in range(3)])
            inside = [
                [~above[0][0], None],
                [above[0][0] & ~above[0][1], ~above[1][1]],
                [above[0][1] & ~above[0][2], above[1][1] & ~above[1][2]],
                [None, above[1][2]],
            ]
            inside[1][1] = ~above[1][1] & above[1][0]
            for number in range(4):
                first_half, second_half = inside[number]
                if second_half is None:
                    chosen = [jnp.where(first_half, corr[0][part], zero) for part in range(2)]
                    strength = jnp.where(first_half, power[0], zero)
                elif first_half is None:
                    chosen = [jnp.where(second_half, corr[1][part], zero) for part in range(2)]
                    strength = jnp.where(second_half, power[1], zero)
                else:
                    chosen = [
                        jnp.where(
                            first_half, corr[0][part], jnp.where(second_half, corr[1][part], zero)
                        )
                        for part in range(2)
                    ]
                    strength = jnp.where(first_half, power[0], zero) + jnp.where(
                        second_half, power[1], zero
                    )
                for part in range(2):
                    masked[number, there, part * quarter : (part + 1) * quarter] = chosen[
                        part
                    ].astype(jnp.bfloat16)
                folded = strength[0:8]
                for start in range(8, step, 8):
                    folded = folded + strength[start : start + 8]
                sums[number] += folded

        for index in range(SIDE // step):
            correlate(index)

        def first_pass(number, tile):
            product = jnp.dot(
                masked[number],
                third_ref[number, :, 2 * tile * 128 : 2 * (tile + 1) * 128],
                preferred_element_type=jnp.float32,
            ).reshape(HALF // step, 2, step, 2 * 128)
            lanes = slice(tile * 128, (tile + 1) * 128)
            real, imag = [], []
            for half in range(2):
                old_real, old_imag = (
                    product[:, half, :, part * 128 : (part + 1) * 128].astype(jnp.bfloat16)
                    for part in range(2)
                )
                cosine, sine = (
                    phase_ref[kind, half * HALF : (half + 1) * HALF, lanes].reshape(
                        HALF // step, step, 128
                    )
                    for kind in range(2)
                )
                real.append(old_real * cosine - old_imag * sine)
                imag.append(old_real * sine + old_imag * cosine)
            for part, (upper, lower) in enumerate((real, imag)):
                rows = slice(part * HALF, (part + 1) * HALF)
                columns = slice(number * 128, (number + 1) * 128)
                for parity, value in enumerate((upper + lower, upper - lower)):
                    turned[parity, tile, rows, columns] = value.reshape(HALF, 128)

        for number in range(4):
            for tile in range(SIDE // 128):
                first_pass(number, tile)

        bin_power = [jnp.sum(sums[number]) for number in range(4)]
        total = (bin_power[0] + bin_power[1]) + (bin_power[2] + bin_power[3])
        total_row = jnp.full((1, 128), total, jnp.float32)
        shares = [
            jnp.full((1, 128), bin_power[number], jnp.float32) / total_row for number in range(4)
        ]
        scale = (1.0 / LENGTH) / total_row

        def second_pass(tile, parity):
            product = jnp.dot(
                fourth_ref[parity], turned[parity, tile], preferred_element_type=jnp.float32
            ).reshape(quarter // 8, 2, 8, 4 * 128)
            real, imag = (
                [product[:, part, :, number * 128 : (number + 1) * 128] for number in range(4)]
                for part in range(2)
            )
            sum_real = (real[0] + real[1]) + (real[2] + real[3])
            sum_imag = (imag[0] + imag[1]) + (imag[2] + imag[3])
            square = (sum_real * sum_real + sum_imag * sum_imag) * scale
            snr = square * lax.rsqrt(jnp.maximum(square, TINY))
            chisq = None
            for number in range(4):
                diff_real = real[number] - shares[number] * sum_real
                diff_imag = imag[number] - shares[number] * sum_imag
                term = diff_real * diff_real + diff_imag * diff_imag
                chisq = term if chisq is None else chisq + term
            chisq = chisq * scale
            reduced = chisq * (1.0 / 6.0)
            reduced = jnp.maximum(reduced, 1.0)
            inner = 0.5 + 0.5 * (reduced * reduced * reduced)
            newsnr = snr * jnp.exp2(jnp.log2(inner) * (-1.0 / 6.0))
            for kind, value in enumerate((snr, chisq)):
                rows = value.reshape(quarter, 128)
                for row in range(quarter):
                    place = (row * 2 * (SIDE // 128) + parity * (SIDE // 128) + tile) * 128
                    (snr_ref, chisq_ref)[kind][0, :, place : place + 128] = rows[
                        row : row + 1
                    ].astype(jnp.bfloat16)
            return jnp.max(newsnr.reshape(quarter, 128), axis=0, keepdims=True)

        peak = jnp.zeros((1, 128), jnp.float32)
        for tile in range(SIDE // 128):
            for parity in range(2):
                peak = jnp.maximum(peak, second_pass(tile, parity))
        peak_ref[...] = jnp.max(peak, axis=1, keepdims=True)

    vmem = pl.BlockSpec(memory_space=pltpu.VMEM)
    return pl.pallas_call(
        body,
        out_shape=(
            jax.ShapeDtypeStruct((1, 1, LENGTH // 2), jnp.bfloat16),
            jax.ShapeDtypeStruct((1, 1, LENGTH // 2), jnp.bfloat16),
            jax.ShapeDtypeStruct((1, 1), jnp.float32),
        ),
        in_specs=[vmem] * (5 + n_blocks),
        out_specs=(vmem, vmem, vmem),
        scratch_shapes=[
            pltpu.VMEM((2, HALF, SIDE), jnp.bfloat16),
            pltpu.VMEM((SIDE, SIDE), jnp.bfloat16),
            pltpu.VMEM((4, SIDE, HALF), jnp.bfloat16),
            pltpu.VMEM((2, SIDE // 128, SIDE, 4 * 128), jnp.bfloat16),
            pltpu.VMEM((4, 8, quarter), jnp.float32),
        ],
        compiler_params=pltpu.CompilerParams(vmem_limit_bytes=16 * MIB),
        name="inverse",
    )(spectrum, *blocks, *in_vmem(edges, third, fourth, phase))


def exchange(value, mesh_shape, mask_of):
    groups, segments, cores = (mesh_shape[name] for name in AXES)
    pairs = []
    for group in range(groups):
        for segment in range(segments):
            for core in range(cores):
                here = (group * segments + segment) * cores + core
                other = segment ^ mask_of(core)
                pairs.append((here, (group * segments + other) * cores + core))
    return lax.ppermute(value, AXES, pairs)


def arrange_plain(strain_frames, frame_slot):
    count = lax.axis_size("segment")
    position = lax.axis_index("segment")
    frame_length = strain_frames.shape[1]
    counter = jnp.arange(count, dtype=jnp.int32)
    slot_now = lax.dynamic_slice_in_dim(frame_slot, position, 1, 1)[:, 0]
    next_index = jnp.minimum(position + 1, count - 1)
    slot_next = lax.dynamic_slice_in_dim(frame_slot, next_index, 1, 1)[:, 0]

    def arrange(slots, frames):
        selector = (counter[:, None] == slots[None, :]).astype(jnp.bfloat16)
        placed = jnp.dot(selector, frames, preferred_element_type=jnp.float32)
        return placed.astype(jnp.bfloat16).reshape(HALF, SIDE)

    following_rows = jnp.concatenate(
        [strain_frames[1:], jnp.zeros((1, frame_length), jnp.bfloat16)], axis=0
    )
    outgoing = jnp.stack([strain_frames, following_rows], axis=1)
    received = lax.all_to_all(outgoing, "segment", split_axis=0, concat_axis=0, tiled=True)
    leading = arrange(slot_now, received[:, 0])
    trailing = arrange(slot_next, received[:, 1])
    return jnp.concatenate([leading, trailing])


def local(mesh_shape, strain_frames, frame_slot, templates, bin_edges):
    constants = tables()
    count = mesh_shape["segment"]
    rows = strain_frames.shape[1] // SIDE
    staged = count == 8 and mesh_shape["template"] == 2 and rows % 16 == 0
    if staged:
        across = exchange(templates, mesh_shape, lambda core: 4)
        *outgoing, mine, unpacked = split_frames(strain_frames, templates)
        received = [
            exchange(value, mesh_shape, functools.partial(strain_mask, step))
            for step, value in enumerate(outgoing)
        ]
        pair = pair_shards(unpacked, across)
        near = exchange(pair, mesh_shape, lambda core: 1 + core)
        first, second, third, fourth, phase, factors = constants
        first, factors = load_tables((first, factors), pair)
        *received, first = lax.optimization_barrier((*received, first))
        other = lax.ppermute(jnp.stack(received), "template", [(0, 1), (1, 0)])
        far = exchange(jnp.concatenate([pair, near]), mesh_shape, lambda core: 2 - core)
        blocks = [pair, near, far]
        spectrum = forward_received(received, other, mine, frame_slot, first, second, factors)
    else:
        first, second, third, fourth, phase, factors = constants
        signal = arrange_plain(strain_frames, frame_slot)
        whole = lax.all_gather(templates, "segment", axis=2, tiled=True)
        blocks = [whole.reshape(1, 2, HALF, SIDE)]
        spectrum = forward_arranged(signal, first, second, factors)
    return inverse(spectrum, blocks, bin_edges, third, fourth, phase, staged)


def solution(mesh):
    mesh_shape = dict(mesh.shape)

    def step(strain_frames, frame_slot, templates, bin_edges):
        return local(mesh_shape, strain_frames, frame_slot, templates, bin_edges)

    in_specs = (
        P("segment", None),
        P(),
        P(("groups", "template"), None, "segment"),
        P(("groups", "template"), None),
    )
    out_specs = (
        P("segment", ("groups", "template"), None),
        P("segment", ("groups", "template"), None),
        P("segment", ("groups", "template")),
    )
    return jax.shard_map(step, mesh=mesh, in_specs=in_specs, out_specs=out_specs, check_vma=False)
```
